256 devices in a mesh: seq: 32 (over z, x_lo, core), head: 8 (over x_hi, y).
Axes of the slice: x: 4 (x_hi: 2, x_lo: 2; x = x_hi * 2 + x_lo), y: 4, z: 8, core: 2. Of those that a mesh axis runs over, the one named last changes fastest.
Arguments:
- queries: bfloat16 [8192, 2048], P('seq', 'head'), may hold values from -6 to 6
- key_vectors: bfloat16 [8192, 2048], P('seq', 'head'), may hold values from -6 to 6
- value_vectors: bfloat16 [8192, 2048], P('seq', 'head'), may hold values from -3 to 3
- group_order: int32 [64], replicated, may hold values from 0 to 63, each once
- doc_lengths: int32 [8], replicated, may hold values from 1 to 3072, 8192 in all
- out_grad: bfloat16 [8192, 4096], P('seq'), may hold values from -2.09375 to 2.09375
- out_weight: bfloat16 [2048, 4096], P('head'), may hold values from -0.125 to 0.125
Outputs:
- layer_out: bfloat16 [8192, 4096], P('seq', 'head')
- grad_queries: bfloat16 [8192, 2048], P('seq', 'head')
- grad_keys: bfloat16 [8192, 2048], P('seq', 'head')
- grad_values: bfloat16 [8192, 2048], P('seq', 'head')
The draws below stay inside these ranges and needn't reach their ends.
Inputs may be any that keep to these rules, and one draw needn't show every extreme that they name: `group_order`: every group number appears exactly once. `doc_lengths`: the lengths sum to 8192; the longest is exactly 3072.
All inputs are finite; a program needn't handle non-finite values.
Results may differ from the reference program's by a relative error of at most 0.03.
Values may be sent and summed in bfloat16 or wider, within the bound.
A program may use at most 128 MiB of HBM per device.

```python
import math
import jax
import jax.numpy as jnp
import numpy as np
from jax import lax

D = 4096
HEADS = 16
HD = 128
SEQ = 8192
GROUP = 128
DOCS = 8
LONGEST = 3072
N_SEQ = 32


def draw_queries(key, part):
    key = jax.random.fold_in(key, 5)
    drawn = jnp.clip(jax.random.normal(key, (SEQ, HEADS * HD), jnp.float32), -4.0, 4.0)
    return drawn.astype(jnp.bfloat16)


def draw_key_vectors(key, part):
    key = jax.random.fold_in(key, 9)
    drawn = jnp.clip(jax.random.normal(key, (SEQ, HEADS * HD), jnp.float32), -4.0, 4.0)
    return drawn.astype(jnp.bfloat16)


def steps_of(stream_key, dims, shards, low, largest):
    def one(dim, blocks):
        draws = jax.random.uniform(jax.random.fold_in(jax.random.fold_in(stream_key, 6), dim), (blocks,), jnp.float32, low / len(shards), largest / len(shards))
        return jnp.repeat(jnp.exp(draws), dims[dim] // blocks).reshape((-1,) + (1,) * (len(dims) - dim - 1))

    factor_of = one(*shards[0])
    for cut in shards[1:]:
        factor_of = factor_of * one(*cut)
    return factor_of


def split_up(amount, total, most, lean):
    loads = [(1 << 20) // math.isqrt(rank ** lean) + 1 for rank in range(2, amount + 1)]
    surplus, holding = total - most - (amount - 1), [1] * (amount - 1)
    while surplus > 0:
        free = [i for i in range(amount - 1) if holding[i] < most]
        pool, remaining = sum([loads[i] for i in free]), surplus
        for i in free:
            addition = min(most - holding[i], max(1, remaining * loads[i] // pool), surplus)
            holding[i] = holding[i] + addition
            surplus = surplus - addition
    return np.array([most] + holding)


def uneven(own_key, count, total, reach, slope):
    if count == 2:
        one = jax.random.randint(own_key, (), max(1, total - reach), min(reach, total - 1) + 1)
        return jnp.stack([one, total - one])
    tallies = jnp.asarray(split_up(count, total, reach, slope), jnp.int32)
    couples = (count - 1) // 2
    giver, receiver = tallies[1:1 + 2 * couples:2], tallies[2:2 + 2 * couples:2]
    room = jnp.minimum(giver - 1, reach - receiver)
    passed = jax.random.randint(jax.random.fold_in(own_key, 1), (couples,), 0, 1 << 20) % (room + 1)
    tallies = tallies.at[1:1 + 2 * couples:2].set(giver - passed).at[2:2 + 2 * couples:2].set(receiver + passed)
    return tallies[jax.random.permutation(jax.random.fold_in(own_key, 2), count)]


def bell_draw(stream_key, extent, width, most, cuts=(), kind=jnp.bfloat16):
    gain = steps_of(stream_key, extent, cuts, -0.22, 0.18) if cuts else 1.0
    values = jax.random.normal(stream_key, extent, jnp.float32) * width * gain
    return jnp.minimum(jnp.maximum(values, -most), most).astype(kind)


def setup_inputs(seed: int = 0) -> dict:
    keys = jax.random.split(jax.random.key(seed), 8)
    return {
        "queries": draw_queries(jax.random.fold_in(keys[7], 71), 0),
        "key_vectors": draw_key_vectors(jax.random.fold_in(keys[7], 71), 0),
        "value_vectors": bell_draw(keys[2], (SEQ, HEADS * HD), 0.5, 3.0, ((0, 32), (1, 8))),
        "group_order": jax.random.permutation(keys[3], 2 * N_SEQ).astype(jnp.int32),
        "doc_lengths": uneven(keys[4], DOCS, SEQ, LONGEST, 2).astype(jnp.int32),
        "out_grad": bell_draw(keys[5], (SEQ, D), 0.35, 2.09375, ((0, 32),)),
        "out_weight": bell_draw(keys[6], (HEADS * HD, D), (HEADS * HD) ** -0.5, 0.125, ((0, 8),)),
    }


EXCLUDED = -1e+30

def narrowed(array):
    return lax.optimization_barrier(array.astype(jnp.bfloat16))

def token_positions(group_order):
    row_ids = jnp.arange(SEQ, dtype=jnp.int32)
    return (group_order[row_ids // GROUP] * GROUP + row_ids % GROUP).astype(jnp.int32)

def documents(position, doc_lengths):
    doc_ends = jnp.cumsum(doc_lengths).astype(jnp.int32)
    return lax.optimization_barrier(jnp.sum((position[:, None] >= doc_ends[None, :]).astype(jnp.int32), axis=1))

def split_heads(array):
    return array.reshape(SEQ, HEADS, HD).transpose(1, 0, 2)

def reference(queries, key_vectors, value_vectors, group_order, doc_lengths, out_grad, out_weight):
    position = token_positions(group_order)
    document = documents(position, doc_lengths)
    visible = (position[None, :] <= position[:, None]) & (document[None, :] == document[:, None])
    score_scale = 1.0 / math.sqrt(HD)

    def head_logits(query_head, key_head):
        logits = jnp.dot(query_head.astype(jnp.float32), key_head.astype(jnp.float32).T) * score_scale
        return jnp.where(visible, logits, EXCLUDED)

    def forward(head_data):
        query_head, key_head, value_head = head_data
        logits = head_logits(query_head, key_head)
        row_max = lax.optimization_barrier(jnp.max(logits, axis=1))
        exps = jnp.where(visible, jnp.exp(logits - row_max[:, None]), 0.0)
        total = lax.optimization_barrier(jnp.sum(exps, axis=1))
        log_total = row_max + jnp.log(total)
        weights = narrowed(exps)
        attention = jnp.dot(weights.astype(jnp.float32), value_head.astype(jnp.float32)) / total[:, None]
        return (attention.astype(jnp.bfloat16), log_total)
    query_heads = split_heads(queries)
    key_heads = split_heads(key_vectors)
    value_heads = split_heads(value_vectors)
    attn_heads, log_totals = lax.map(forward, (query_heads, key_heads, value_heads))
    attention = lax.optimization_barrier(attn_heads.transpose(1, 0, 2).reshape(SEQ, HEADS * HD))
    layer_out = jnp.dot(attention.astype(jnp.float32), out_weight.astype(jnp.float32)).astype(jnp.bfloat16)
    d_attention = narrowed(jnp.dot(out_grad.astype(jnp.float32), out_weight.astype(jnp.float32).T))
    grad_heads = split_heads(d_attention)
    attn_split = split_heads(attention)

    def backward(head_data):
        query_head, key_head, value_head, attn_head, grad_head, log_total = head_data
        logits = head_logits(query_head, key_head)
        row_delta = lax.optimization_barrier(jnp.sum(grad_head.astype(jnp.float32) * attn_head.astype(jnp.float32), axis=1))
        probs_full = jnp.where(visible, jnp.exp(logits - log_total[:, None]), 0.0)
        probs_low = narrowed(probs_full)
        value_grad = jnp.dot(probs_low.astype(jnp.float32).T, grad_head.astype(jnp.float32))
        dprobs = jnp.dot(grad_head.astype(jnp.float32), value_head.astype(jnp.float32).T)
        dscores = narrowed(probs_full * (dprobs - row_delta[:, None]) * score_scale)
        query_grad = jnp.dot(dscores.astype(jnp.float32), key_head.astype(jnp.float32))
        key_grad = jnp.dot(dscores.astype(jnp.float32).T, query_head.astype(jnp.float32))
        return (query_grad.astype(jnp.bfloat16), key_grad.astype(jnp.bfloat16), value_grad.astype(jnp.bfloat16))
    query_grads, key_grads, value_grads = lax.map(backward, (query_heads, key_heads, value_heads, attn_split, grad_heads, log_totals))

    def merge_heads(array):
        return array.transpose(1, 0, 2).reshape(SEQ, HEADS * HD)
    return (layer_out, merge_heads(query_grads), merge_heads(key_grads), merge_heads(value_grads))
```

```python
import functools
import math

import jax
import jax.numpy as jnp
from jax import lax
from jax.experimental import pallas as pl
from jax.experimental.pallas import tpu as pltpu
from jax.sharding import PartitionSpec as P

HD = 128
GROUP = 128
DOCS = 8
NZ = 8
NK = 8
BLK = 512
HALF = 256
PAIR = 2 * BLK
TILE = 256
SCALE = 1.0 / math.sqrt(HD)
HIDDEN = -1e30
LOWEST = -5e29
F32 = jnp.float32
BF16 = jnp.bfloat16
MESH = pl.DeviceIdType.MESH


def dot_nt(a, b):
    return lax.dot_general(a, b, (((1,), (1,)), ((), ())), preferred_element_type=F32)


def dot_nn(a, b):
    return jnp.dot(a, b, preferred_element_type=F32)


def kernel(
    order, lengths, q_in, k_in, v_in, og_hbm, w_hbm,
    layer_out, dq_out, dk_out, dv_out,
    xk, xv, xq, xg,
    og, wfull, wg, da, da_acc, att, attg,
    first, place, last,
    o_acc, m_acc, l_acc, lse_col, delta_col, dq_acc, dk_acc, dv_acc,
    o_send, o_recv, st_send, st_recv, st_z, st_par, grad_send, grad_recv,
    send_sem, recv_sem, local_sem,
):
    s = lax.axis_index("seq")
    k = lax.axis_index("head")
    core = s % 2
    other = 1 - core
    x = (s // 2) % 2
    z = s // 4
    sibling = s + 1 - 2 * core
    partner = s + 2 - 4 * x
    diagonal = partner + 1 - 2 * core

    def z_peer(e):
        return ((z + e) % NZ) * 4 + s % 4

    def seq_dev(t):
        return (t, k)

    def head_dev(e):
        return (s, (k + e) % NK)

    def weight_dev(e):
        kk = (k + e) % NK
        diff = (kk // 4 - k // 4) * (kk // 4 - k // 4)
        return (s + diff * (2 - 4 * x), kk)

    load_w = pltpu.make_async_copy(w_hbm, wfull, local_sem.at[0])
    load_g = pltpu.make_async_copy(og_hbm, og, local_sem.at[1])
    load_w.start()
    load_g.start()

    barrier = pltpu.get_barrier_semaphore()
    targets = [seq_dev(sibling), seq_dev(partner), seq_dev(diagonal)]
    targets += [seq_dev(z_peer(e)) for e in range(1, NZ)]
    targets += [head_dev(e) for e in range(1, NK)]
    targets += [weight_dev(e) for e in range(1, NK)]
    for t in targets:
        pl.semaphore_signal(barrier, inc=1, device_id=t, device_id_type=MESH)

    own_cols = pl.ds(pl.multiple_of(core * HD, HD), HD)
    other_cols = pl.ds(pl.multiple_of(other * HD, HD), HD)
    half_rows = (pl.multiple_of(core * HALF, HALF), pl.multiple_of(other * HALF, HALF))

    def rows_of(block, j):
        return pl.ds(pl.multiple_of(block * BLK + half_rows[j], HALF), HALF)

    own_rows = rows_of(1, 0)
    xq[own_rows, :] = q_in[:, own_cols]
    xk[own_rows, :] = k_in[:, own_cols]
    xv[own_rows, :] = v_in[:, own_cols]
    pl.semaphore_wait(barrier, len(targets))

    counter = [0]
    pending = []

    def remote(src, dst, target):
        n = counter[0]
        counter[0] += 1
        copy = pltpu.make_async_remote_copy(
            src_ref=src, dst_ref=dst, send_sem=send_sem.at[n], recv_sem=recv_sem.at[n],
            device_id=target, device_id_type=MESH,
        )
        copy.start()
        pending.append(copy)
        return copy

    def ring_send(arr, block_from, block_to, j, e):
        return remote(
            arr.at[rows_of(block_from, j), :], arr.at[rows_of(block_to, j), :], seq_dev(z_peer(e))
        )

    ring = {}

    def ring_start(name, arr, j):
        ring[name, 1, j] = ring_send(arr, 1, 2, j, 1)
        ring[name, 7, j] = ring_send(arr, 1, 8, j, NZ - 1)

    def ring_service(named, t):
        for name, arr in named:
            for j in (0, 1):
                for sign in (1, -1):
                    d = t if sign == 1 else NZ - t
                    ring[name, d, j].wait_recv()
                    if t < 3 or (t == 3 and (j == 0) == (sign == 1)):
                        e = 1 if sign == 1 else NZ - 1
                        ring[name, d + sign, j] = ring_send(arr, 1 + d, 1 + d + sign, j, e)

    def ring_last(named):
        for name, arr in named:
            for j in (0, 1):
                ring[name, 4, j].wait_recv()

    def to_sibling(src, arr):
        return remote(src.at[:, other_cols], arr.at[rows_of(1, 0), :], seq_dev(sibling))

    def to_pair(src, arr):
        return (
            remote(src.at[:, own_cols], arr.at[rows_of(0, 0), :], seq_dev(partner)),
            remote(src.at[:, other_cols], arr.at[rows_of(0, 0), :], seq_dev(diagonal)),
        )

    kv = (("k", xk), ("v", xv))
    qg = (("q", xq), ("g", xg))

    sib_k = to_sibling(k_in, xk)
    ring_start("k", xk, 0)
    sib_v = to_sibling(v_in, xv)
    ring_start("v", xv, 0)
    sib_q = to_sibling(q_in, xq)
    pair_q = to_pair(q_in, xq)
    sib_k.wait_recv()
    ring_start("k", xk, 1)
    sib_v.wait_recv()
    ring_start("v", xv, 1)

    ends = []
    total = jnp.int32(0)
    for j in range(DOCS):
        total = total + lengths[j]
        ends.append(total)

    def chip_group(zz, xx):
        return zz * 8 + xx * 4

    lane = lax.broadcasted_iota(jnp.int32, (GROUP, GROUP), 1)
    sub = lax.broadcasted_iota(jnp.int32, (GROUP, GROUP), 0)

    def place_body(g, _):
        xx = jnp.where(g < 4, 1 - x, x)
        pos = order[chip_group(z, xx) + g % 4] * GROUP + sub
        low = jnp.zeros((GROUP, GROUP), jnp.int32)
        high = jnp.full((GROUP, GROUP), 1 << 29, jnp.int32)
        for e in ends:
            low = jnp.maximum(low, jnp.where(pos >= e, e, 0))
            high = jnp.minimum(high, jnp.where(pos < e, e, 1 << 29))
        rows = pl.ds(pl.multiple_of(g * GROUP, GROUP), GROUP)
        first[rows, :] = low - lane
        place[rows, :] = pos - lane
        last[rows, :] = high - 1 - lane
        return 0

    lax.fori_loop(0, 8, place_body, 0)

    def base(d, j):
        return order[chip_group((z + NZ - d) % NZ, x) + j] * GROUP

    m_acc[...] = jnp.full((PAIR, HD), LOWEST, F32)
    l_acc[...] = jnp.zeros((PAIR, HD), F32)
    o_acc[...] = jnp.zeros((PAIR, HD), F32)
    dq_acc[...] = jnp.zeros((PAIR, HD), F32)
    dk_acc[...] = jnp.zeros((PAIR, HD), F32)
    dv_acc[...] = jnp.zeros((PAIR, HD), F32)

    def block_rows(d, n=1):
        return pl.ds((1 + d) * BLK, n * BLK)

    load_w.wait()
    load_g.wait()
    da_acc[...] = jnp.zeros((HALF, HALF), F32)

    def da_body(i, _):
        cols = pl.ds(pl.multiple_of(i * 1024, 1024), 1024)
        da_acc[...] += dot_nt(og[:, cols], wfull[:, cols])
        return 0

    lax.fori_loop(0, 4, da_body, 0)
    da[...] = da_acc[...].astype(BF16)
    xg[own_rows, :] = da[:, own_cols]
    sib_g = to_sibling(da, xg)

    col_half = pl.ds(pl.multiple_of(core * 256, 256), 256)
    w_copies = []
    for e in range(1, NK):
        kk = (k + e) % NK
        src = wfull.at[:, pl.ds(pl.multiple_of(kk * 512 + core * 256, 256), 256)]
        w_copies.append(remote(src, wg.at[k, :, col_half], weight_dev(e)))
    wg[k, :, :] = wfull[:, pl.ds(pl.multiple_of(k * 512, 512), 512)]

    pair_k = to_pair(k_in, xk)
    pair_v = to_pair(v_in, xv)

    def forward(blocks):
        def body(i, _):
            rows = pl.ds(pl.multiple_of(i * TILE, TILE), TILE)
            q = xq[rows, :]
            low, high = first[rows, :], place[rows, :]
            parts = []
            for d in blocks:
                logits = dot_nt(q, xk[block_rows(d), :])
                for j in range(4):
                    b = base(d, j)
                    part = logits[:, j * GROUP:(j + 1) * GROUP] * SCALE
                    parts.append(jnp.where((low <= b) & (high >= b), part, HIDDEN))
            top = functools.reduce(jnp.maximum, parts)
            old = m_acc[rows, :]
            new = jnp.maximum(old, jnp.max(top, axis=1, keepdims=True))
            factor = jnp.exp(old - new)
            weights = [jnp.exp(part - new) for part in parts]
            l_acc[rows, :] = l_acc[rows, :] * factor + functools.reduce(jnp.add, weights)
            m_acc[rows, :] = new
            product = o_acc[rows, :] * factor
            for n, d in enumerate(blocks):
                low_w = jnp.concatenate([w.astype(BF16) for w in weights[4 * n:4 * n + 4]], axis=1)
                product = product + dot_nn(low_w, xv[block_rows(d), :])
            o_acc[rows, :] = product
            return 0

        lax.fori_loop(0, PAIR // TILE, body, 0)

    sib_q.wait_recv()
    for c in pair_q:
        c.wait_recv()
    forward((0,))
    sib_g.wait_recv()
    pair_g = to_pair(da, xg)
    for t in (1, 2, 3):
        ring_service(kv, t)
        if t == 3:
            for j in (0, 1):
                ring_start("q", xq, j)
                ring_start("g", xg, j)
        forward((t, NZ - t))
    ring_last(kv)
    forward((4,))

    def close(rows):
        totals = jnp.maximum(jnp.sum(l_acc[rows, :], axis=1, keepdims=True), 1e-30)
        totals = jnp.broadcast_to(totals, (BLK, HD))
        return o_acc[rows, :] / totals, m_acc[rows, :] + jnp.log(totals)

    o_part, lse_part = close(pl.ds(0, BLK))
    o_send[...] = o_part.astype(BF16)
    st_send[0, :, :] = lse_part.T[0:8, :]
    copy_o = remote(o_send, o_recv, seq_dev(partner))
    copy_l = remote(st_send.at[0], st_recv, seq_dev(partner))
    ring_service(qg, 1)

    w_sib = []
    for e in range(1, NK):
        w_copies[e - 1].wait_recv()
        ref = wg.at[(k + NK - e) % NK, :, col_half]
        w_sib.append(remote(ref, ref, seq_dev(sibling)))

    o_own, lse_own = close(pl.ds(BLK, BLK))
    copy_l.wait_recv()
    copy_o.wait_recv()

    def to_col(row):
        return jnp.broadcast_to(row, (HD, BLK)).T

    lse_other = to_col(st_recv[0:1, :])
    top = jnp.maximum(lse_own, lse_other)
    lse = top + jnp.log(jnp.exp(lse_own - top) + jnp.exp(lse_other - top))
    merged = o_own * jnp.exp(lse_own - lse) + o_recv[...].astype(F32) * jnp.exp(lse_other - lse)
    attention = merged.astype(BF16)
    att[...] = attention
    delta = jnp.sum(
        attention.astype(F32) * xg[block_rows(0), :].astype(F32), axis=1, keepdims=True
    )
    delta = jnp.broadcast_to(delta, (BLK, HD))
    lse_col[BLK:, :] = lse
    delta_col[BLK:, :] = delta
    row8 = lax.broadcasted_iota(jnp.int32, (8, BLK), 0)
    stats = jnp.where(row8 == 0, lse.T[0:8, :], delta.T[0:8, :])
    st_z[0, :, :] = stats
    copy_sp = remote(st_z.at[0], st_par, seq_dev(partner))
    copy_sz = [remote(st_z.at[0], st_z.at[e], seq_dev(z_peer(e))) for e in range(1, NZ)]
    copy_a = remote(
        att.at[pl.ds(half_rows[1], HALF), :], attg.at[k, :, own_cols], seq_dev(sibling)
    )
    attg[k, :, own_cols] = att[pl.ds(half_rows[0], HALF), :]

    def query_side(u0, u1):
        def body(n, _):
            i, u = n % (PAIR // TILE), n // (PAIR // TILE)
            rows = pl.ds(pl.multiple_of(i * TILE, TILE), TILE)
            keys = pl.ds(pl.multiple_of(BLK + u * PAIR, BLK), PAIR)
            low, high = first[rows, :], place[rows, :]
            log_t, dlt = lse_col[rows, :], delta_col[rows, :]
            key = xk[keys, :]
            logits = dot_nt(xq[rows, :], key)
            dprobs = dot_nt(xg[rows, :], xv[keys, :])
            out = []
            for j in range(8):
                b = base(2 * u + j // 4, j % 4)
                cols = slice(j * GROUP, (j + 1) * GROUP)
                part = jnp.where(
                    (low <= b) & (high >= b), logits[:, cols] * SCALE - log_t, HIDDEN
                )
                out.append((jnp.exp(part) * (dprobs[:, cols] - dlt)).astype(BF16))
            dq_acc[rows, :] += dot_nn(jnp.concatenate(out, axis=1), key)
            return 0

        lax.fori_loop(u0 * (PAIR // TILE), u1 * (PAIR // TILE), body, 0)

    def key_side(blocks):
        def body(i, _):
            keys = pl.ds(pl.multiple_of(i * TILE, TILE), TILE)
            low, high = place[keys, :], last[keys, :]
            key, value = xk[keys, :], xv[keys, :]
            dk, dv = dk_acc[keys, :], dv_acc[keys, :]
            for d in blocks:
                query, grad = xq[block_rows(d), :], xg[block_rows(d), :]
                logits = dot_nt(key, query)
                dprobs = dot_nt(value, grad)
                probs, scores = [], []
                for j in range(4):
                    b = base(d, j)
                    cols = slice(j * GROUP, (j + 1) * GROUP)
                    log_t = st_z[d, 0:1, cols]
                    dlt = st_z[d, 1:2, cols]
                    part = jnp.where(
                        (low <= b) & (high >= b), logits[:, cols] * SCALE - log_t, HIDDEN
                    )
                    prob = jnp.exp(part)
                    probs.append(prob.astype(BF16))
                    scores.append((prob * (dprobs[:, cols] - dlt)).astype(BF16))
                dv = dv + dot_nn(jnp.concatenate(probs, axis=1), grad)
                dk = dk + dot_nn(jnp.concatenate(scores, axis=1), query)
            dk_acc[keys, :] = dk
            dv_acc[keys, :] = dv
            return 0

        lax.fori_loop(0, PAIR // TILE, body, 0)

    def send_grad(n, acc, scale):
        def piece(block, j):
            return (acc[rows_of(block, j), :] * scale).astype(BF16)

        copies = []
        for m, (block, j, t) in enumerate(((1, 1, sibling), (0, 0, partner), (0, 1, diagonal))):
            grad_send[n, m, :, :] = piece(block, j)
            copies.append(remote(grad_send.at[n, m], grad_recv.at[n, m], seq_dev(t)))
        return copies

    def finish_grad(n, acc, scale, copies, out):
        for c in copies:
            c.wait_recv()
        mine = acc[rows_of(1, 0), :] * scale + grad_recv[n, 1, :, :].astype(F32)
        theirs = grad_recv[n, 0, :, :].astype(F32) + grad_recv[n, 2, :, :].astype(F32)
        out[:, own_cols] = mine.astype(BF16)
        out[:, other_cols] = theirs.astype(BF16)

    ring_service(qg, 2)
    for c in pair_k + pair_v + pair_g:
        c.wait_recv()
    copy_a.wait_recv()
    att_copies = [remote(attg.at[k], attg.at[k], head_dev(e)) for e in range(1, NK)]
    key_side((0,))
    copy_sp.wait_recv()
    lse_col[:BLK, :] = to_col(st_par[0:1, :])
    delta_col[:BLK, :] = to_col(st_par[1:2, :])
    query_side(0, 2)
    ring_service(qg, 3)
    query_side(2, 4)
    grads_q = send_grad(0, dq_acc, SCALE)
    for c in copy_sz:
        c.wait_recv()
    key_side((1, 7))
    key_side((2, 6))

    for c in att_copies + w_sib:
        c.wait_recv()

    def project(i, total):
        return total + dot_nn(attg[i, :, :], wg[i, :, :])

    layer_out[...] = lax.fori_loop(0, NK, project, jnp.zeros((HALF, 512), F32)).astype(BF16)

    key_side((3, 5))
    ring_last(qg)
    key_side((4,))
    grads_k = send_grad(1, dk_acc, SCALE)
    grads_v = send_grad(2, dv_acc, 1.0)
    finish_grad(0, dq_acc, SCALE, grads_q, dq_out)
    finish_grad(1, dk_acc, SCALE, grads_k, dk_out)
    finish_grad(2, dv_acc, 1.0, grads_v, dv_out)
    for c in pending:
        c.wait_send()


COPIES = 128


def per_device(queries, key_vectors, value_vectors, group_order, doc_lengths, out_grad, out_weight):
    vmem = pl.BlockSpec(memory_space=pltpu.VMEM)
    smem = pl.BlockSpec(memory_space=pltpu.SMEM)
    hbm = pl.BlockSpec(memory_space=pl.ANY)
    blocks = pltpu.VMEM((9 * BLK, HD), BF16)
    pair_f32 = pltpu.VMEM((PAIR, HD), F32)
    pair_int = pltpu.VMEM((PAIR, HD), jnp.int32)
    return pl.pallas_call(
        kernel,
        out_shape=(
            jax.ShapeDtypeStruct((HALF, 512), BF16),
            jax.ShapeDtypeStruct((HALF, 2 * HD), BF16),
            jax.ShapeDtypeStruct((HALF, 2 * HD), BF16),
            jax.ShapeDtypeStruct((HALF, 2 * HD), BF16),
        ),
        in_specs=[smem, smem, vmem, vmem, vmem, hbm, hbm],
        out_specs=(vmem, vmem, vmem, vmem),
        scratch_shapes=[
            blocks, blocks, blocks, blocks,
            pltpu.VMEM((HALF, 4096), BF16),
            pltpu.VMEM((HALF, 4096), BF16),
            pltpu.VMEM((NK, HALF, 512), BF16),
            pltpu.VMEM((HALF, HALF), BF16),
            pltpu.VMEM((HALF, HALF), F32),
            pltpu.VMEM((BLK, HD), BF16),
            pltpu.VMEM((NK, HALF, HALF), BF16),
            pair_int, pair_int, pair_int,
            pair_f32, pair_f32, pair_f32, pair_f32, pair_f32, pair_f32, pair_f32, pair_f32,
            pltpu.VMEM((BLK, HD), BF16),
            pltpu.VMEM((BLK, HD), BF16),
            pltpu.VMEM((1, 8, BLK), F32),
            pltpu.VMEM((8, BLK), F32),
            pltpu.VMEM((NZ, 8, BLK), F32),
            pltpu.VMEM((8, BLK), F32),
            pltpu.VMEM((3, 3, HALF, HD), BF16),
            pltpu.VMEM((3, 3, HALF, HD), BF16),
            pltpu.SemaphoreType.DMA((COPIES,)),
            pltpu.SemaphoreType.DMA((COPIES,)),
            pltpu.SemaphoreType.DMA((2,)),
        ],
        compiler_params=pltpu.CompilerParams(
            collective_id=0, has_side_effects=True, vmem_limit_bytes=48 * 1024 * 1024
        ),
        name="attention_grads",
    )(group_order, doc_lengths, queries, key_vectors, value_vectors, out_grad, out_weight)


def solution(mesh):
    return jax.shard_map(
        per_device,
        mesh=mesh,
        in_specs=(
            P("seq", "head"),
            P("seq", "head"),
            P("seq", "head"),
            P(),
            P(),
            P("seq", None),
            P("head", None),
        ),
        out_specs=(P("seq", "head"), P("seq", "head"), P("seq", "head"), P("seq", "head")),
        check_vma=False,
    )
```

```python
import functools
import math

import jax
import jax.numpy as jnp
from jax import lax
from jax.experimental import pallas as pl
from jax.experimental.pallas import tpu as pltpu
from jax.sharding import PartitionSpec as P

HD = 128
GROUP = 128
DOCS = 8
NZ = 8
NK = 8
BLK = 512
HALF = 256
PAIR = 2 * BLK
KEYS, VALUES, QUERIES, GRADS = range(4)
LOG2E = math.log2(math.e)
SCALE = 1.0 / math.sqrt(HD)
SCALE2 = SCALE * LOG2E
HIDDEN = -1e30
LOWEST = -5e29
F32 = jnp.float32
BF16 = jnp.bfloat16
MESH = pl.DeviceIdType.MESH


def dot_nt(a, b):
    return lax.dot_general(a, b, (((1,), (1,)), ((), ())), preferred_element_type=F32)


def dot_nn(a, b):
    return jnp.dot(a, b, preferred_element_type=F32)


def kernel(
    order_hbm, lengths_hbm, q_hbm, k_hbm, v_hbm, og_hbm, w_hbm,
    layer_hbm, dq_hbm, dk_hbm, dv_hbm,
    order, lengths, q_in, k_in, v_in, layer_out, grad_out,
    xa,
    og, wfull, wg, da, da_acc, att, attg,
    first, place, last,
    o_acc, m_acc, l_acc, a1_acc, a2_acc, dq_acc, dk_acc, dv_acc,
    o_send, o_recv, st_send, st_recv, st_z, st_par, grad_send, grad_recv,
    send_sem, recv_sem, ring_send_sem, ring_recv_sem, stat_send_sem, stat_recv_sem, local_sem,
):
    s = lax.axis_index("seq")
    k = lax.axis_index("head")
    core = s % 2
    other = 1 - core
    x = (s // 2) % 2
    z = s // 4
    sibling = s + 1 - 2 * core
    partner = s + 2 - 4 * x
    diagonal = partner + 1 - 2 * core

    def z_peer(e):
        return ((z + e) % NZ) * 4 + s % 4

    def seq_dev(t):
        return (t, k)

    def head_dev(e):
        return (s, (k + e) % NK)

    def weight_dev(e):
        kk = (k + e) % NK
        diff = (kk // 4 - k // 4) * (kk // 4 - k // 4)
        return (s + diff * (2 - 4 * x), kk)

    barrier = pltpu.get_barrier_semaphore()
    targets = [seq_dev(sibling), seq_dev(partner), seq_dev(diagonal)]
    targets += [seq_dev(z_peer(e)) for e in range(1, NZ)]
    targets += [head_dev(e) for e in range(1, NK)]
    targets += [weight_dev(e) for e in range(1, NK)]
    for t in targets:
        pl.semaphore_signal(barrier, inc=1, device_id=t, device_id_type=MESH)

    def local(src, dst, n):
        copy = pltpu.make_async_copy(src, dst, local_sem.at[n])
        copy.start()
        return copy

    loads = [
        local(src, dst, n)
        for n, (src, dst) in enumerate((
            (order_hbm, order), (lengths_hbm, lengths),
            (k_hbm, k_in), (v_hbm, v_in), (q_hbm, q_in), (w_hbm, wfull), (og_hbm, og),
        ))
    ]

    own_cols = pl.ds(pl.multiple_of(core * HD, HD), HD)
    other_cols = pl.ds(pl.multiple_of(other * HD, HD), HD)
    xk, xv, xq, xg = (xa.at[a] for a in (KEYS, VALUES, QUERIES, GRADS))
    half_rows = (pl.multiple_of(core * HALF, HALF), pl.multiple_of(other * HALF, HALF))

    def rows_of(block, j):
        return pl.ds(pl.multiple_of(block * BLK + half_rows[j], HALF), HALF)

    for c in loads[:2]:
        c.wait()
    ends = []
    total = jnp.int32(0)
    for j in range(DOCS):
        total = total + lengths[j]
        ends.append(total)

    def chip_group(zz, xx):
        return zz * 8 + xx * 4

    lane = lax.broadcasted_iota(jnp.int32, (GROUP, GROUP), 1)
    sub = lax.broadcasted_iota(jnp.int32, (GROUP, GROUP), 0)

    def place_body(g, _):
        xx = jnp.where(g < 4, 1 - x, x)
        pos = order[chip_group(z, xx) + g % 4] * GROUP + sub
        low = jnp.zeros((GROUP, GROUP), jnp.int32)
        high = jnp.full((GROUP, GROUP), 1 << 29, jnp.int32)
        for e in ends:
            low = jnp.maximum(low, jnp.where(pos >= e, e, 0))
            high = jnp.minimum(high, jnp.where(pos < e, e, 1 << 29))
        rows = pl.ds(pl.multiple_of(g * GROUP, GROUP), GROUP)
        first[rows, :] = low - lane
        place[rows, :] = pos - lane
        last[rows, :] = high - 1 - lane
        return 0

    lax.fori_loop(0, 8, place_body, 0)

    def base(d, j):
        return order[chip_group((z + NZ - d) % NZ, x) + j] * GROUP

    own_rows = rows_of(1, 0)
    for c in loads[2:5]:
        c.wait()
    xk[own_rows, :] = k_in[:, own_cols]
    xv[own_rows, :] = v_in[:, own_cols]
    xq[own_rows, :] = q_in[:, own_cols]
    m_acc[...] = jnp.full((PAIR, HD), LOWEST, F32)
    for acc in (l_acc, o_acc, a1_acc, a2_acc, dk_acc, dv_acc):
        acc[...] = jnp.zeros((PAIR, HD), F32)

    for c in loads[5:]:
        c.wait()
    da_acc[...] = jnp.zeros((HALF, HALF), F32)

    def da_body(i, _):
        cols = pl.ds(pl.multiple_of(i * 1024, 1024), 1024)
        da_acc[...] += dot_nt(og[:, cols], wfull[:, cols])
        return 0

    lax.fori_loop(0, 4, da_body, 0)
    da[...] = da_acc[...].astype(BF16)
    xg[own_rows, :] = da[:, own_cols]

    pl.semaphore_wait(barrier, len(targets))

    counter = [0]
    pending = []

    def plan(src, dst, target):
        n = counter[0]
        counter[0] += 1
        copy = pltpu.make_async_remote_copy(
            src_ref=src, dst_ref=dst, send_sem=send_sem.at[n], recv_sem=recv_sem.at[n],
            device_id=target, device_id_type=MESH,
        )
        pending.append(copy)
        return copy

    def remote(src, dst, target):
        copy = plan(src, dst, target)
        copy.start()
        return copy

    def ring_copy(a, back, t, j):
        src, dst = (1 + (9 - t) % NZ, 9 - t) if back else (t, 1 + t)
        return pltpu.make_async_remote_copy(
            src_ref=xa.at[a, rows_of(src, j), :], dst_ref=xa.at[a, rows_of(dst, j), :],
            send_sem=ring_send_sem.at[a, back, t - 1, j],
            recv_sem=ring_recv_sem.at[a, back, t - 1, j],
            device_id=seq_dev(z_peer(NZ - 1 if back else 1)), device_id_type=MESH,
        )

    def ring_start(a, j):
        for back in (0, 1):
            ring_copy(a, back, 1, j).start()

    def ring_service(a, t):
        for j in (0, 1):
            for back in (0, 1):
                if j == back:
                    ring_copy(a, back, t, j).wait_recv()

                    @pl.when(t < 4)
                    def _():
                        ring_copy(a, back, t + 1, j).start()
                else:
                    @pl.when(t < 4)
                    def _():
                        ring_copy(a, back, t, j).wait_recv()

                    @pl.when(t < 3)
                    def _():
                        ring_copy(a, back, t + 1, j).start()

    def to_sibling(src, arr):
        return remote(src.at[:, other_cols], arr.at[rows_of(1, 0), :], seq_dev(sibling))

    def to_pair(src, arr):
        return (
            remote(src.at[:, own_cols], arr.at[rows_of(0, 0), :], seq_dev(partner)),
            remote(src.at[:, other_cols], arr.at[rows_of(0, 0), :], seq_dev(diagonal)),
        )

    sib_k = to_sibling(k_in, xk)
    sib_v = to_sibling(v_in, xv)
    ring_start(KEYS, 0)
    ring_start(VALUES, 0)
    sib_q = to_sibling(q_in, xq)
    sib_g = to_sibling(da, xg)
    pair_q = to_pair(q_in, xq)
    pair_g = to_pair(da, xg)
    sib_k.wait_recv()
    ring_start(KEYS, 1)
    sib_v.wait_recv()
    ring_start(VALUES, 1)
    pair_k = to_pair(k_in, xk)
    pair_v = to_pair(v_in, xv)

    col_half = pl.ds(pl.multiple_of(core * 256, 256), 256)
    w_copies = []
    for e in range(1, NK):
        kk = (k + e) % NK
        src = wfull.at[:, pl.ds(pl.multiple_of(kk * 512 + core * 256, 256), 256)]
        w_copies.append(remote(src, wg.at[k, :, col_half], weight_dev(e)))
    wg[k, :, :] = wfull[:, pl.ds(pl.multiple_of(k * 512, 512), 512)]
    w_sib = []
    for e in range(1, NK):
        ref = wg.at[(k + NK - e) % NK, :, col_half]
        w_sib.append(plan(ref, ref, seq_dev(sibling)))

    copy_l = plan(st_send.at[0], st_recv, seq_dev(partner))
    copy_o = plan(o_send, o_recv, seq_dev(partner))
    att_copies = [plan(attg.at[k], attg.at[k], head_dev(e)) for e in range(1, NK)]
    grads = [
        [
            plan(grad_send.at[n, m], grad_recv.at[n, m], seq_dev(t))
            for m, t in enumerate((sibling, partner, diagonal))
        ]
        for n in range(3)
    ]

    def block_rows(d):
        return pl.ds(pl.multiple_of((1 + d) * BLK, BLK), BLK)

    def pair_of(p):
        return ((NZ - p) % NZ, p + 1)

    own, theirs = pl.ds(BLK, BLK), pl.ds(0, BLK)

    def forward(blocks, rows):
        q, grad = xq[rows, :], xg[rows, :]
        low, high = first[rows, :], place[rows, :]
        parts, dprobs = [], []
        for d in blocks:
            logits = dot_nt(q, xk[block_rows(d), :])
            dprobs.append(dot_nt(grad, xv[block_rows(d), :]))
            for j in range(4):
                b = base(d, j)
                part = logits[:, j * GROUP:(j + 1) * GROUP] * SCALE2
                parts.append(jnp.where((low <= b) & (high >= b), part, HIDDEN))
        top = functools.reduce(jnp.maximum, parts)
        old = m_acc[rows, :]
        new = jnp.maximum(old, jnp.max(top, axis=1, keepdims=True))
        factor = jnp.exp2(old - new)
        weights = [jnp.exp2(part - new) for part in parts]
        l_acc[rows, :] = l_acc[rows, :] * factor + functools.reduce(jnp.add, weights)
        m_acc[rows, :] = new
        o_sum = o_acc[rows, :] * factor
        a1_sum = a1_acc[rows, :] * factor
        a2_sum = a2_acc[rows, :] * factor
        for n, d in enumerate(blocks):
            key = xk[block_rows(d), :]
            mine = weights[4 * n:4 * n + 4]
            both = dot_nn(
                jnp.concatenate([w.astype(BF16) for w in mine], axis=1),
                jnp.concatenate([xv[block_rows(d), :], key], axis=1),
            )
            o_sum = o_sum + both[:, :HD]
            a2_sum = a2_sum + both[:, HD:]
            scores = [
                (w * dprobs[n][:, j * GROUP:(j + 1) * GROUP]).astype(BF16)
                for j, w in enumerate(mine)
            ]
            a1_sum = a1_sum + dot_nn(jnp.concatenate(scores, axis=1), key)
        o_acc[rows, :] = o_sum
        a1_acc[rows, :] = a1_sum
        a2_acc[rows, :] = a2_sum

    def close(rows):
        totals = jnp.maximum(jnp.sum(l_acc[rows, :], axis=1, keepdims=True), 1e-30)
        totals = jnp.broadcast_to(totals, (BLK, HD))
        return o_acc[rows, :] / totals, m_acc[rows, :] + jnp.log(totals) * LOG2E

    for c in (sib_q, sib_g) + pair_q + pair_g:
        c.wait_recv()
    ring_service(KEYS, 1)

    def forward_step(n, _):
        p = n // 2

        @pl.when(n < 7)
        def _():
            ring_service(1 - n % 2, (n + 1) // 2 + 1)

        @pl.when(n == 4)
        def _():
            for a in (QUERIES, GRADS):
                for j in (0, 1):
                    ring_start(a, j)

        @pl.when(n == 7)
        def _():
            o_part, lse_part = close(theirs)
            o_send[...] = o_part.astype(BF16)
            st_send[0, :, :] = lse_part.T[0:8, :]
            copy_l.start()
            copy_o.start()

        forward(pair_of(p), pl.ds(pl.multiple_of((n % 2) * BLK, BLK), BLK))
        return 0

    lax.fori_loop(0, 8, forward_step, 0)
    ring_service(QUERIES, 1)
    o_own, lse_own = close(own)
    ring_service(GRADS, 1)
    copy_l.wait_recv()
    copy_o.wait_recv()

    def to_col(row):
        return jnp.broadcast_to(row, (HD, BLK)).T

    lse_other = to_col(st_recv[0:1, :])
    top = jnp.maximum(lse_own, lse_other)
    lse = top + jnp.log(jnp.exp2(lse_own - top) + jnp.exp2(lse_other - top)) * LOG2E
    merged = o_own * jnp.exp2(lse_own - lse) + o_recv[...].astype(F32) * jnp.exp2(lse_other - lse)
    attention = merged.astype(BF16)
    att[...] = attention
    delta = jnp.sum(
        attention.astype(F32) * xg[block_rows(0), :].astype(F32), axis=1, keepdims=True
    )
    delta = jnp.broadcast_to(delta, (BLK, HD))
    row8 = lax.broadcasted_iota(jnp.int32, (8, BLK), 0)
    st_z[0, :, :] = jnp.where(row8 == 0, lse.T[0:8, :], delta.T[0:8, :])
    def stats_copy(e):
        return pltpu.make_async_remote_copy(
            src_ref=st_z.at[0], dst_ref=st_z.at[e],
            send_sem=stat_send_sem.at[e], recv_sem=stat_recv_sem.at[e],
            device_id=seq_dev(z_peer(e)), device_id_type=MESH,
        )

    for e in (1, 7, 2, 6, 3, 5, 4):
        stats_copy(e).start()
    copy_sp = remote(st_z.at[0], st_par, seq_dev(partner))
    copy_a = remote(
        att.at[pl.ds(half_rows[1], HALF), :], attg.at[k, :, own_cols], seq_dev(sibling)
    )
    attg[k, :, own_cols] = att[pl.ds(half_rows[0], HALF), :]

    def close_queries(rows, lse_rows, delta_rows):
        factor = jnp.exp2(m_acc[rows, :] - lse_rows) * SCALE
        dq_acc[rows, :] = (a1_acc[rows, :] - delta_rows * a2_acc[rows, :]) * factor

    def key_side(blocks, keys):
        low, high = place[keys, :], last[keys, :]
        key, value = xk[keys, :], xv[keys, :]
        dk, dv = dk_acc[keys, :], dv_acc[keys, :]
        for d in blocks:
            query, grad = xq[block_rows(d), :], xg[block_rows(d), :]
            logits = dot_nt(key, query)
            dprobs = dot_nt(value, grad)
            probs, scores = [], []
            for j in range(4):
                b = base(d, j)
                cols = slice(j * GROUP, (j + 1) * GROUP)
                log_t = st_z[d, 0:1, cols]
                dlt = st_z[d, 1:2, cols]
                part = jnp.where(
                    (low <= b) & (high >= b), logits[:, cols] * SCALE2 - log_t, HIDDEN
                )
                prob = jnp.exp2(part)
                probs.append(prob.astype(BF16))
                scores.append((prob * (dprobs[:, cols] - dlt)).astype(BF16))
            dv = dv + dot_nn(jnp.concatenate(probs, axis=1), grad)
            dk = dk + dot_nn(jnp.concatenate(scores, axis=1), query)
        dk_acc[keys, :] = dk
        dv_acc[keys, :] = dv

    def send_grad(n, acc, scale, m):
        block, j = ((1, 1), (0, 0), (0, 1))[m]
        grad_send[n, m, :, :] = (acc[rows_of(block, j), :] * scale).astype(BF16)
        grads[n][m].start()

    def finish_grad(n, acc, scale, out):
        for c in grads[n]:
            c.wait_recv()
        mine = acc[rows_of(1, 0), :] * scale + grad_recv[n, 1, :, :].astype(F32)
        not_mine = grad_recv[n, 0, :, :].astype(F32) + grad_recv[n, 2, :, :].astype(F32)
        grad_out[n, :, own_cols] = mine.astype(BF16)
        grad_out[n, :, other_cols] = not_mine.astype(BF16)
        return local(grad_out.at[n], out, 7 + n)

    close_queries(own, lse, delta)
    for c in pair_k + pair_v:
        c.wait_recv()

    def key_step(n, _):
        p = n // 2

        @pl.when(n > 0)
        def _():
            @pl.when(n < 7)
            def _():
                ring_service(3 - n % 2, (n + 1) // 2 + 1)

        @pl.when(n % 2 == 0)
        def _():
            stats_copy(p + 1).wait_recv()

            @pl.when(p > 0)
            def _():
                stats_copy(NZ - p).wait_recv()

        @pl.when(n == 1)
        def _():
            copy_a.wait_recv()
            for c in att_copies:
                c.start()
            copy_sp.wait_recv()
            close_queries(theirs, to_col(st_par[0:1, :]), to_col(st_par[1:2, :]))
            for m in (1, 2, 0):
                send_grad(0, dq_acc, 1.0, m)

        @pl.when(n == 2)
        def _():
            for c, d in zip(w_copies, w_sib):
                c.wait_recv()
                d.start()

        @pl.when(n == 7)
        def _():
            for m in (1, 2):
                send_grad(2, dv_acc, 1.0, m)
                send_grad(1, dk_acc, SCALE, m)

        key_side(pair_of(p), pl.ds(pl.multiple_of((n % 2) * BLK, BLK), BLK))
        return 0

    lax.fori_loop(0, 8, key_step, 0)
    send_grad(2, dv_acc, 1.0, 0)
    send_grad(1, dk_acc, SCALE, 0)
    stores = [finish_grad(0, dq_acc, 1.0, dq_hbm)]

    for c in att_copies + w_sib:
        c.wait_recv()

    def project(i, total):
        return total + dot_nn(attg[i, :, :], wg[i, :, :])

    layer_out[...] = lax.fori_loop(0, NK, project, jnp.zeros((HALF, 512), F32)).astype(BF16)
    stores.append(local(layer_out, layer_hbm, 10))
    stores.append(finish_grad(2, dv_acc, 1.0, dv_hbm))
    stores.append(finish_grad(1, dk_acc, SCALE, dk_hbm))
    for c in stores:
        c.wait()
    for c in pending:
        c.wait_send()
    for e in range(1, NZ):
        stats_copy(e).wait_send()

    def drain(a, _):
        for j in (0, 1):
            for back in (0, 1):
                for t in range(1, 5 if j == back else 4):
                    ring_copy(a, back, t, j).wait_send()
        return 0

    lax.fori_loop(0, 4, drain, 0)


COPIES = 56
VMEM_BYTES = 62 * 1024 * 1024


def emit(a, b, c, d, a_out, b_out, c_out, d_out, a_buf, b_buf, c_buf, d_buf, sem):
    steps = ((a, a_buf, a_out), (b, b_buf, b_out), (c, c_buf, c_out), (d, d_buf, d_out))
    loads = [pltpu.make_async_copy(t[0], t[1], sem.at[0, n]) for n, t in enumerate(steps)]
    stores = [pltpu.make_async_copy(t[1], t[2], sem.at[1, n]) for n, t in enumerate(steps)]
    for copy in loads:
        copy.start()
    for load, store in zip(loads, stores):
        load.wait()
        store.start()
    for copy in stores:
        copy.wait()


def per_device(queries, key_vectors, value_vectors, group_order, doc_lengths, out_grad, out_weight):
    hbm = pl.BlockSpec(memory_space=pl.ANY)
    local = pltpu.VMEM((HALF, 2 * HD), BF16)
    pair_f32 = pltpu.VMEM((PAIR, HD), F32)
    pair_int = pltpu.VMEM((PAIR, HD), jnp.int32)
    results = pl.pallas_call(
        kernel,
        out_shape=(
            jax.ShapeDtypeStruct((HALF, 512), BF16),
            jax.ShapeDtypeStruct((HALF, 2 * HD), BF16),
            jax.ShapeDtypeStruct((HALF, 2 * HD), BF16),
            jax.ShapeDtypeStruct((HALF, 2 * HD), BF16),
        ),
        in_specs=[hbm] * 7,
        out_specs=(hbm, hbm, hbm, hbm),
        scratch_shapes=[
            pltpu.SMEM((64,), jnp.int32),
            pltpu.SMEM((DOCS,), jnp.int32),
            local, local, local,
            pltpu.VMEM((HALF, 512), BF16),
            pltpu.VMEM((3, HALF, 2 * HD), BF16),
            pltpu.VMEM((4, 9 * BLK, HD), BF16),
            pltpu.VMEM((HALF, 4096), BF16),
            pltpu.VMEM((HALF, 4096), BF16),
            pltpu.VMEM((NK, HALF, 512), BF16),
            pltpu.VMEM((HALF, HALF), BF16),
            pltpu.VMEM((HALF, HALF), F32),
            pltpu.VMEM((BLK, HD), BF16),
            pltpu.VMEM((NK, HALF, HALF), BF16),
            pair_int, pair_int, pair_int,
            pair_f32, pair_f32, pair_f32, pair_f32, pair_f32, pair_f32, pair_f32, pair_f32,
            pltpu.VMEM((BLK, HD), BF16),
            pltpu.VMEM((BLK, HD), BF16),
            pltpu.VMEM((1, 8, BLK), F32),
            pltpu.VMEM((8, BLK), F32),
            pltpu.VMEM((NZ, 8, BLK), F32),
            pltpu.VMEM((8, BLK), F32),
            pltpu.VMEM((3, 3, HALF, HD), BF16),
            pltpu.VMEM((3, 3, HALF, HD), BF16),
            pltpu.SemaphoreType.DMA((COPIES,)),
            pltpu.SemaphoreType.DMA((COPIES,)),
            pltpu.SemaphoreType.DMA((4, 2, 4, 2)),
            pltpu.SemaphoreType.DMA((4, 2, 4, 2)),
            pltpu.SemaphoreType.DMA((NZ,)),
            pltpu.SemaphoreType.DMA((NZ,)),
            pltpu.SemaphoreType.DMA((11,)),
        ],
        compiler_params=pltpu.CompilerParams(
            collective_id=0, has_side_effects=True, vmem_limit_bytes=VMEM_BYTES
        ),
        name="attention_grads",
    )(group_order, doc_lengths, queries, key_vectors, value_vectors, out_grad, out_weight)
    return pl.pallas_call(
        emit,
        out_shape=tuple(jax.ShapeDtypeStruct(r.shape, r.dtype) for r in results),
        in_specs=[pl.BlockSpec(memory_space=pl.ANY)] * 4,
        out_specs=(pl.BlockSpec(memory_space=pl.ANY),) * 4,
        scratch_shapes=[pltpu.VMEM(r.shape, r.dtype) for r in results]
        + [pltpu.SemaphoreType.DMA((2, 4))],
        compiler_params=pltpu.CompilerParams(vmem_limit_bytes=VMEM_BYTES),
        name="emit",
    )(*results)


def solution(mesh):
    return jax.shard_map(
        per_device,
        mesh=mesh,
        in_specs=(
            P("seq", "head"),
            P("seq", "head"),
            P("seq", "head"),
            P(),
            P(),
            P("seq", None),
            P("head", None),
        ),
        out_specs=(P("seq", "head"), P("seq", "head"), P("seq", "head"), P("seq", "head")),
        check_vma=False,
    )
```

```python
import functools
import math

import jax
import jax.numpy as jnp
from jax import lax
from jax.experimental import pallas as pl
from jax.experimental.pallas import tpu as pltpu
from jax.sharding import PartitionSpec as P

HD = 128
GROUP = 128
DOCS = 8
NZ = 8
NK = 8
BLK = 512
HALF = 256
PAIR = 2 * BLK
KEYS, VALUES, QUERIES, GRADS = range(4)
LOG2E = math.log2(math.e)
SCALE = 1.0 / math.sqrt(HD)
SCALE2 = SCALE * LOG2E
HIDDEN = -1e30
LOWEST = -5e29
F32 = jnp.float32
BF16 = jnp.bfloat16
MESH = pl.DeviceIdType.MESH


def dot_nt(a, b):
    return lax.dot_general(a, b, (((1,), (1,)), ((), ())), preferred_element_type=F32)


def dot_nn(a, b):
    return jnp.dot(a, b, preferred_element_type=F32)


def kernel(
    order_hbm, lengths_hbm, q_hbm, k_hbm, v_hbm, og_hbm, w_hbm,
    layer_hbm, dq_hbm, dk_hbm, dv_hbm,
    order, lengths, q_in, k_in, v_in, layer_out, grad_out,
    xa,
    og, wfull, wg, da, da_acc, att, attg,
    first, place, last,
    o_acc, m_acc, l_acc, a1_acc, a2_acc, dq_acc, dk_acc, dv_acc,
    o_send, o_recv, st_send, st_recv, st_z, st_par, grad_send, grad_recv,
    send_sem, recv_sem, ring_send_sem, ring_recv_sem, stat_send_sem, stat_recv_sem, local_sem,
):
    s = lax.axis_index("seq")
    k = lax.axis_index("head")
    core = s % 2
    other = 1 - core
    x = (s // 2) % 2
    z = s // 4
    sibling = s + 1 - 2 * core
    partner = s + 2 - 4 * x
    diagonal = partner + 1 - 2 * core

    def z_peer(e):
        return ((z + e) % NZ) * 4 + s % 4

    def seq_dev(t):
        return (t, k)

    def row_dev(e):
        return (s, k - k % 4 + (k + e) % 4)

    k_far = (k + 4) % NK
    far_dev = (s, k_far)

    def weight_dev(e):
        kk = (k + e) % NK
        diff = (kk // 4 - k // 4) * (kk // 4 - k // 4)
        return (s + diff * (2 - 4 * x), kk)

    barrier = pltpu.get_barrier_semaphore()
    targets = [seq_dev(sibling), seq_dev(partner), seq_dev(diagonal)]
    targets += [seq_dev(z_peer(e)) for e in (1, NZ - 1)]
    targets += [row_dev(e) for e in range(1, 4)] + [far_dev]
    targets += [weight_dev(e) for e in range(1, NK)]
    for t in targets:
        pl.semaphore_signal(barrier, inc=1, device_id=t, device_id_type=MESH)

    def local(src, dst, n):
        copy = pltpu.make_async_copy(src, dst, local_sem.at[n])
        copy.start()
        return copy

    loads = [
        local(src, dst, n)
        for n, (src, dst) in enumerate((
            (order_hbm, order), (lengths_hbm, lengths),
            (k_hbm, k_in), (v_hbm, v_in), (q_hbm, q_in), (w_hbm, wfull), (og_hbm, og),
        ))
    ]

    own_cols = pl.ds(pl.multiple_of(core * HD, HD), HD)
    other_cols = pl.ds(pl.multiple_of(other * HD, HD), HD)
    xk, xv, xq, xg = (xa.at[a] for a in (KEYS, VALUES, QUERIES, GRADS))
    half_rows = (pl.multiple_of(core * HALF, HALF), pl.multiple_of(other * HALF, HALF))

    def rows_of(block, j):
        return pl.ds(pl.multiple_of(block * BLK + half_rows[j], HALF), HALF)

    for c in loads[:2]:
        c.wait()
    ends = []
    total = jnp.int32(0)
    for j in range(DOCS):
        total = total + lengths[j]
        ends.append(total)

    def chip_group(zz, xx):
        return zz * 8 + xx * 4

    lane = lax.broadcasted_iota(jnp.int32, (GROUP, GROUP), 1)
    sub = lax.broadcasted_iota(jnp.int32, (GROUP, GROUP), 0)

    def place_body(g, _):
        xx = jnp.where(g < 4, 1 - x, x)
        pos = order[chip_group(z, xx) + g % 4] * GROUP + sub
        low = jnp.zeros((GROUP, GROUP), jnp.int32)
        high = jnp.full((GROUP, GROUP), 1 << 29, jnp.int32)
        for e in ends:
            low = jnp.maximum(low, jnp.where(pos >= e, e, 0))
            high = jnp.minimum(high, jnp.where(pos < e, e, 1 << 29))
        rows = pl.ds(pl.multiple_of(g * GROUP, GROUP), GROUP)
        first[rows, :] = low - lane
        place[rows, :] = pos - lane
        last[rows, :] = high - 1 - lane
        return 0

    lax.fori_loop(0, 8, place_body, 0)

    def base(d, j):
        return order[chip_group((z + NZ - d) % NZ, x) + j] * GROUP

    own_rows = rows_of(1, 0)
    for c in loads[2:5]:
        c.wait()
    xk[own_rows, :] = k_in[:, own_cols]
    xv[own_rows, :] = v_in[:, own_cols]
    xq[own_rows, :] = q_in[:, own_cols]
    m_acc[...] = jnp.full((PAIR, HD), LOWEST, F32)
    for acc in (l_acc, o_acc, a1_acc, a2_acc, dk_acc, dv_acc):
        acc[...] = jnp.zeros((PAIR, HD), F32)

    for c in loads[5:]:
        c.wait()
    da_acc[...] = jnp.zeros((HALF, HALF), F32)

    def da_body(i, _):
        cols = pl.ds(pl.multiple_of(i * 1024, 1024), 1024)
        da_acc[...] += dot_nt(og[:, cols], wfull[:, cols])
        return 0

    lax.fori_loop(0, 4, da_body, 0)
    da[...] = da_acc[...].astype(BF16)
    xg[own_rows, :] = da[:, own_cols]

    pl.semaphore_wait(barrier, len(targets))

    counter = [0]
    pending = []

    def plan(src, dst, target):
        n = counter[0]
        counter[0] += 1
        copy = pltpu.make_async_remote_copy(
            src_ref=src, dst_ref=dst, send_sem=send_sem.at[n], recv_sem=recv_sem.at[n],
            device_id=target, device_id_type=MESH,
        )
        pending.append(copy)
        return copy

    def remote(src, dst, target):
        copy = plan(src, dst, target)
        copy.start()
        return copy

    def ring_copy(a, back, t, j):
        src, dst = (1 + (9 - t) % NZ, 9 - t) if back else (t, 1 + t)
        return pltpu.make_async_remote_copy(
            src_ref=xa.at[a, rows_of(src, j), :], dst_ref=xa.at[a, rows_of(dst, j), :],
            send_sem=ring_send_sem.at[a, back, t - 1, j],
            recv_sem=ring_recv_sem.at[a, back, t - 1, j],
            device_id=seq_dev(z_peer(NZ - 1 if back else 1)), device_id_type=MESH,
        )

    def ring_start(a, j):
        for back in (0, 1):
            ring_copy(a, back, 1, j).start()

    def ring_service(a, t):
        for j in (0, 1):
            for back in (0, 1):
                if j == back:
                    ring_copy(a, back, t, j).wait_recv()

                    @pl.when(t < 4)
                    def _():
                        ring_copy(a, back, t + 1, j).start()
                else:
                    @pl.when(t < 4)
                    def _():
                        ring_copy(a, back, t, j).wait_recv()

                    @pl.when(t < 3)
                    def _():
                        ring_copy(a, back, t + 1, j).start()

    def to_sibling(src, arr):
        return remote(src.at[:, other_cols], arr.at[rows_of(1, 0), :], seq_dev(sibling))

    def to_pair(src, arr):
        return (
            remote(src.at[:, own_cols], arr.at[rows_of(0, 0), :], seq_dev(partner)),
            remote(src.at[:, other_cols], arr.at[rows_of(0, 0), :], seq_dev(diagonal)),
        )

    sib_k = to_sibling(k_in, xk)
    sib_v = to_sibling(v_in, xv)
    ring_start(KEYS, 0)
    ring_start(VALUES, 0)
    sib_q = to_sibling(q_in, xq)
    sib_g = to_sibling(da, xg)
    pair_q = to_pair(q_in, xq)
    pair_g = to_pair(da, xg)
    sib_k.wait_recv()
    ring_start(KEYS, 1)
    sib_v.wait_recv()
    ring_start(VALUES, 1)
    pair_k = to_pair(k_in, xk)
    pair_v = to_pair(v_in, xv)
    ring_service(KEYS, 1)

    col_half = pl.ds(pl.multiple_of(core * 256, 256), 256)
    w_copies = []
    for e in range(1, NK):
        kk = (k + e) % NK
        src = wfull.at[:, pl.ds(pl.multiple_of(kk * 512 + core * 256, 256), 256)]
        w_copies.append(remote(src, wg.at[k, :, col_half], weight_dev(e)))
    wg[k, :, :] = wfull[:, pl.ds(pl.multiple_of(k * 512, 512), 512)]
    w_sib = []
    for e in range(1, NK):
        ref = wg.at[(k + NK - e) % NK, :, col_half]
        w_sib.append(plan(ref, ref, seq_dev(sibling)))

    copy_l = plan(st_send.at[0], st_recv, seq_dev(partner))
    copy_o = plan(o_send, o_recv, seq_dev(partner))
    att_far = plan(attg.at[k], attg.at[k], far_dev)
    att_near = [plan(attg.at[k], attg.at[k], row_dev(e)) for e in range(1, 4)]
    att_relay = [plan(attg.at[k_far], attg.at[k_far], row_dev(e)) for e in range(1, 4)]
    grads = [
        [
            plan(grad_send.at[n, m], grad_recv.at[n, m], seq_dev(t))
            for m, t in enumerate((sibling, partner, diagonal))
        ]
        for n in range(3)
    ]

    def block_rows(d):
        return pl.ds(pl.multiple_of((1 + d) * BLK, BLK), BLK)

    def block_of(i):
        return jnp.where(i % 2 == 1, (i + 1) // 2, (NZ - i // 2) % NZ)

    own, theirs = pl.ds(BLK, BLK), pl.ds(0, BLK)

    def forward(blocks, rows):
        q, grad = xq[rows, :], xg[rows, :]
        low, high = first[rows, :], place[rows, :]
        parts, dprobs = [], []
        for d in blocks:
            logits = dot_nt(q, xk[block_rows(d), :])
            dprobs.append(dot_nt(grad, xv[block_rows(d), :]))
            for j in range(4):
                b = base(d, j)
                part = logits[:, j * GROUP:(j + 1) * GROUP] * SCALE2
                parts.append(jnp.where((low <= b) & (high >= b), part, HIDDEN))
        top = functools.reduce(jnp.maximum, parts)
        old = m_acc[rows, :]
        new = jnp.maximum(old, jnp.max(top, axis=1, keepdims=True))
        factor = jnp.exp2(old - new)
        weights = [jnp.exp2(part - new) for part in parts]
        l_acc[rows, :] = l_acc[rows, :] * factor + functools.reduce(jnp.add, weights)
        m_acc[rows, :] = new
        o_sum = o_acc[rows, :] * factor
        a1_sum = a1_acc[rows, :] * factor
        a2_sum = a2_acc[rows, :] * factor
        for n, d in enumerate(blocks):
            key = xk[block_rows(d), :]
            mine = weights[4 * n:4 * n + 4]
            both = dot_nn(
                jnp.concatenate([w.astype(BF16) for w in mine], axis=1),
                jnp.concatenate([xv[block_rows(d), :], key], axis=1),
            )
            o_sum = o_sum + both[:, :HD]
            a2_sum = a2_sum + both[:, HD:]
            scores = [
                (w * dprobs[n][:, j * GROUP:(j + 1) * GROUP]).astype(BF16)
                for j, w in enumerate(mine)
            ]
            a1_sum = a1_sum + dot_nn(jnp.concatenate(scores, axis=1), key)
        o_acc[rows, :] = o_sum
        a1_acc[rows, :] = a1_sum
        a2_acc[rows, :] = a2_sum

    def close(rows):
        totals = jnp.maximum(jnp.sum(l_acc[rows, :], axis=1, keepdims=True), 1e-30)
        totals = jnp.broadcast_to(totals, (BLK, HD))
        return o_acc[rows, :] / totals, m_acc[rows, :] + jnp.log(totals) * LOG2E

    ring_service(VALUES, 1)
    for c in (sib_q, sib_g) + pair_q + pair_g:
        c.wait_recv()

    def forward_step(n, _):
        @pl.when((n % 2 == 0) & (n >= 4))
        def _():
            ring_service((n // 2) % 2, n // 4 + 1)

        @pl.when(n == 10)
        def _():
            for a in (QUERIES, GRADS):
                for j in (0, 1):
                    ring_start(a, j)

        @pl.when(n == 15)
        def _():
            o_part, lse_part = close(theirs)
            o_send[...] = o_part.astype(BF16)
            st_send[0, :, :] = lse_part.T[0:8, :]
            copy_l.start()
            copy_o.start()

        forward((block_of(n // 2),), pl.ds(pl.multiple_of((n % 2) * BLK, BLK), BLK))
        return 0

    lax.fori_loop(0, 16, forward_step, 0)
    ring_service(QUERIES, 1)
    o_own, lse_own = close(own)
    ring_service(GRADS, 1)
    copy_l.wait_recv()
    copy_o.wait_recv()

    def to_col(row):
        return jnp.broadcast_to(row, (HD, BLK)).T

    lse_other = to_col(st_recv[0:1, :])
    top = jnp.maximum(lse_own, lse_other)
    lse = top + jnp.log(jnp.exp2(lse_own - top) + jnp.exp2(lse_other - top)) * LOG2E
    merged = o_own * jnp.exp2(lse_own - lse) + o_recv[...].astype(F32) * jnp.exp2(lse_other - lse)
    attention = merged.astype(BF16)
    att[...] = attention
    delta = jnp.sum(
        attention.astype(F32) * xg[block_rows(0), :].astype(F32), axis=1, keepdims=True
    )
    delta = jnp.broadcast_to(delta, (BLK, HD))
    row8 = lax.broadcasted_iota(jnp.int32, (8, BLK), 0)
    st_z[0, :, :] = jnp.where(row8 == 0, lse.T[0:8, :], delta.T[0:8, :])
    def stats_copy(back, t):
        src, dst = ((9 - t) % NZ, NZ - t) if back else (t - 1, t)
        return pltpu.make_async_remote_copy(
            src_ref=st_z.at[src], dst_ref=st_z.at[dst],
            send_sem=stat_send_sem.at[back, t - 1], recv_sem=stat_recv_sem.at[back, t - 1],
            device_id=seq_dev(z_peer(NZ - 1 if back else 1)), device_id_type=MESH,
        )

    def stats_service(t):
        stats_copy(0, t).wait_recv()
        stats_copy(0, t + 1).start()
        stats_copy(1, t).wait_recv()

        @pl.when(t < 3)
        def _():
            stats_copy(1, t + 1).start()

    for back in (0, 1):
        stats_copy(back, 1).start()
    copy_sp = remote(st_z.at[0], st_par, seq_dev(partner))
    copy_a = remote(
        att.at[pl.ds(half_rows[1], HALF), :], attg.at[k, :, own_cols], seq_dev(sibling)
    )
    attg[k, :, own_cols] = att[pl.ds(half_rows[0], HALF), :]

    def close_queries(rows, lse_rows, delta_rows):
        factor = jnp.exp2(m_acc[rows, :] - lse_rows) * SCALE
        dq_acc[rows, :] = (a1_acc[rows, :] - delta_rows * a2_acc[rows, :]) * factor

    def key_side(blocks, keys):
        low, high = place[keys, :], last[keys, :]
        key, value = xk[keys, :], xv[keys, :]
        dk, dv = dk_acc[keys, :], dv_acc[keys, :]
        for d in blocks:
            query, grad = xq[block_rows(d), :], xg[block_rows(d), :]
            logits = dot_nt(key, query)
            dprobs = dot_nt(value, grad)
            probs, scores = [], []
            for j in range(4):
                b = base(d, j)
                cols = slice(j * GROUP, (j + 1) * GROUP)
                log_t = st_z[d, 0:1, cols]
                dlt = st_z[d, 1:2, cols]
                part = jnp.where(
                    (low <= b) & (high >= b), logits[:, cols] * SCALE2 - log_t, HIDDEN
                )
                prob = jnp.exp2(part)
                probs.append(prob.astype(BF16))
                scores.append((prob * (dprobs[:, cols] - dlt)).astype(BF16))
            dv = dv + dot_nn(jnp.concatenate(probs, axis=1), grad)
            dk = dk + dot_nn(jnp.concatenate(scores, axis=1), query)
        dk_acc[keys, :] = dk
        dv_acc[keys, :] = dv

    def send_grad(n, acc, scale, m):
        block, j = ((1, 1), (0, 0), (0, 1))[m]
        grad_send[n, m, :, :] = (acc[rows_of(block, j), :] * scale).astype(BF16)
        grads[n][m].start()

    def finish_grad(n, acc, scale, out):
        for c in grads[n]:
            c.wait_recv()
        mine = acc[rows_of(1, 0), :] * scale + grad_recv[n, 1, :, :].astype(F32)
        not_mine = grad_recv[n, 0, :, :].astype(F32) + grad_recv[n, 2, :, :].astype(F32)
        grad_out[n, :, own_cols] = mine.astype(BF16)
        grad_out[n, :, other_cols] = not_mine.astype(BF16)
        return local(grad_out.at[n], out, 7 + n)

    close_queries(own, lse, delta)
    for c in pair_k + pair_v:
        c.wait_recv()

    def key_step(i, _):
        @pl.when((i == 1) | (i == 4))
        def _():
            ring_service(QUERIES, i // 3 + 2)

        @pl.when((i == 2) | (i == 5))
        def _():
            ring_service(GRADS, i // 3 + 2)

        @pl.when(i == 6)
        def _():
            ring_service(QUERIES, 4)

        @pl.when(i % 2 == 1)
        def _():
            stats_service((i + 1) // 2)

        @pl.when(i == 1)
        def _():
            copy_a.wait_recv()
            for c in [att_far] + att_near:
                c.start()

        @pl.when(i == 2)
        def _():
            copy_sp.wait_recv()
            close_queries(theirs, to_col(st_par[0:1, :]), to_col(st_par[1:2, :]))
            for m in (1, 2, 0):
                send_grad(0, dq_acc, 1.0, m)

        @pl.when(i == 3)
        def _():
            for c, d in zip(w_copies, w_sib):
                c.wait_recv()
                d.start()

        @pl.when(i == 5)
        def _():
            att_far.wait_recv()
            for c in att_relay:
                c.start()

        key_side((block_of(i),), pl.ds(0, PAIR))
        return 0

    lax.fori_loop(0, 7, key_step, 0)
    ring_service(GRADS, 4)
    stats_copy(0, 4).wait_recv()

    def last_step(i, _):
        @pl.when(i == 1)
        def _():
            for m in (1, 2):
                send_grad(2, dv_acc, 1.0, m)
                send_grad(1, dk_acc, SCALE, m)

        key_side((4,), pl.ds(pl.multiple_of(i * BLK, BLK), BLK))
        return 0

    lax.fori_loop(0, 2, last_step, 0)
    send_grad(2, dv_acc, 1.0, 0)
    send_grad(1, dk_acc, SCALE, 0)
    stores = [finish_grad(0, dq_acc, 1.0, dq_hbm)]

    for c in att_near + att_relay + w_sib:
        c.wait_recv()

    def project(i, total):
        return total + dot_nn(attg[i, :, :], wg[i, :, :])

    layer_out[...] = lax.fori_loop(0, NK, project, jnp.zeros((HALF, 512), F32)).astype(BF16)
    stores.append(local(layer_out, layer_hbm, 10))
    stores.append(finish_grad(2, dv_acc, 1.0, dv_hbm))
    stores.append(finish_grad(1, dk_acc, SCALE, dk_hbm))
    for c in stores:
        c.wait()
    for c in pending:
        c.wait_send()
    for t in range(1, 5):
        stats_copy(0, t).wait_send()
    for t in range(1, 4):
        stats_copy(1, t).wait_send()

    def drain(a, _):
        for j in (0, 1):
            for back in (0, 1):
                for t in range(1, 5 if j == back else 4):
                    ring_copy(a, back, t, j).wait_send()
        return 0

    lax.fori_loop(0, 4, drain, 0)


COPIES = 56
VMEM_BYTES = 62 * 1024 * 1024


def emit(a, b, c, d, a_out, b_out, c_out, d_out, a_buf, b_buf, c_buf, d_buf, sem):
    steps = ((a, a_buf, a_out), (b, b_buf, b_out), (c, c_buf, c_out), (d, d_buf, d_out))
    loads = [pltpu.make_async_copy(t[0], t[1], sem.at[0, n]) for n, t in enumerate(steps)]
    stores = [pltpu.make_async_copy(t[1], t[2], sem.at[1, n]) for n, t in enumerate(steps)]
    for copy in loads:
        copy.start()
    for load, store in zip(loads, stores):
        load.wait()
        store.start()
    for copy in stores:
        copy.wait()


def per_device(queries, key_vectors, value_vectors, group_order, doc_lengths, out_grad, out_weight):
    hbm = pl.BlockSpec(memory_space=pl.ANY)
    local = pltpu.VMEM((HALF, 2 * HD), BF16)
    pair_f32 = pltpu.VMEM((PAIR, HD), F32)
    pair_int = pltpu.VMEM((PAIR, HD), jnp.int32)
    results = pl.pallas_call(
        kernel,
        out_shape=(
            jax.ShapeDtypeStruct((HALF, 512), BF16),
            jax.ShapeDtypeStruct((HALF, 2 * HD), BF16),
            jax.ShapeDtypeStruct((HALF, 2 * HD), BF16),
            jax.ShapeDtypeStruct((HALF, 2 * HD), BF16),
        ),
        in_specs=[hbm] * 7,
        out_specs=(hbm, hbm, hbm, hbm),
        scratch_shapes=[
            pltpu.SMEM((64,), jnp.int32),
            pltpu.SMEM((DOCS,), jnp.int32),
            local, local, local,
            pltpu.VMEM((HALF, 512), BF16),
            pltpu.VMEM((3, HALF, 2 * HD), BF16),
            pltpu.VMEM((4, 9 * BLK, HD), BF16),
            pltpu.VMEM((HALF, 4096), BF16),
            pltpu.VMEM((HALF, 4096), BF16),
            pltpu.VMEM((NK, HALF, 512), BF16),
            pltpu.VMEM((HALF, HALF), BF16),
            pltpu.VMEM((HALF, HALF), F32),
            pltpu.VMEM((BLK, HD), BF16),
            pltpu.VMEM((NK, HALF, HALF), BF16),
            pair_int, pair_int, pair_int,
            pair_f32, pair_f32, pair_f32, pair_f32, pair_f32, pair_f32, pair_f32, pair_f32,
            pltpu.VMEM((BLK, HD), BF16),
            pltpu.VMEM((BLK, HD), BF16),
            pltpu.VMEM((1, 8, BLK), F32),
            pltpu.VMEM((8, BLK), F32),
            pltpu.VMEM((NZ, 8, BLK), F32),
            pltpu.VMEM((8, BLK), F32),
            pltpu.VMEM((3, 3, HALF, HD), BF16),
            pltpu.VMEM((3, 3, HALF, HD), BF16),
            pltpu.SemaphoreType.DMA((COPIES,)),
            pltpu.SemaphoreType.DMA((COPIES,)),
            pltpu.SemaphoreType.DMA((4, 2, 4, 2)),
            pltpu.SemaphoreType.DMA((4, 2, 4, 2)),
            pltpu.SemaphoreType.DMA((2, 4)),
            pltpu.SemaphoreType.DMA((2, 4)),
            pltpu.SemaphoreType.DMA((11,)),
        ],
        compiler_params=pltpu.CompilerParams(
            collective_id=0, has_side_effects=True, vmem_limit_bytes=VMEM_BYTES
        ),
        name="attention_grads",
    )(group_order, doc_lengths, queries, key_vectors, value_vectors, out_grad, out_weight)
    return pl.pallas_call(
        emit,
        out_shape=tuple(jax.ShapeDtypeStruct(r.shape, r.dtype) for r in results),
        in_specs=[pl.BlockSpec(memory_space=pl.ANY)] * 4,
        out_specs=(pl.BlockSpec(memory_space=pl.ANY),) * 4,
        scratch_shapes=[pltpu.VMEM(r.shape, r.dtype) for r in results]
        + [pltpu.SemaphoreType.DMA((2, 4))],
        compiler_params=pltpu.CompilerParams(vmem_limit_bytes=VMEM_BYTES),
        name="emit",
    )(*results)


def solution(mesh):
    return jax.shard_map(
        per_device,
        mesh=mesh,
        in_specs=(
            P("seq", "head"),
            P("seq", "head"),
            P("seq", "head"),
            P(),
            P(),
            P("seq", None),
            P("head", None),
        ),
        out_specs=(P("seq", "head"), P("seq", "head"), P("seq", "head"), P("seq", "head")),
        check_vma=False,
    )
```

```python
import functools
import math

import jax
import jax.numpy as jnp
from jax import lax
from jax.experimental import pallas as pl
from jax.experimental.pallas import tpu as pltpu
from jax.sharding import PartitionSpec as P

HD = 128
GROUP = 128
DOCS = 8
NZ = 8
NK = 8
BLK = 512
HALF = 256
PAIR = 2 * BLK
KEYS, VALUES, QUERIES, GRADS = range(4)
LOG2E = math.log2(math.e)
SCALE = 1.0 / math.sqrt(HD)
SCALE2 = SCALE * LOG2E
HIDDEN = -1e30
LOWEST = -5e29
F32 = jnp.float32
BF16 = jnp.bfloat16
MESH = pl.DeviceIdType.MESH


def dot_nt(a, b):
    return lax.dot_general(a, b, (((1,), (1,)), ((), ())), preferred_element_type=F32)


def dot_nn(a, b):
    return jnp.dot(a, b, preferred_element_type=F32)


def kernel(
    order_hbm, lengths_hbm, q_hbm, k_hbm, v_hbm, og_hbm, w_hbm,
    layer_hbm, dq_hbm, dk_hbm, dv_hbm,
    order, lengths, q_in, k_in, v_in, layer_out, grad_out,
    xa,
    og, wfull, wg, da, da_acc, att, attg,
    first, place, last,
    o_acc, m_acc, l_acc, a1_acc, a2_acc, dq_acc, dk_acc, dv_acc,
    o_send, o_recv, st_send, st_recv, st_z, st_par, grad_send, grad_recv,
    send_sem, recv_sem, ring_send_sem, ring_recv_sem, stat_send_sem, stat_recv_sem, local_sem,
):
    s = lax.axis_index("seq")
    k = lax.axis_index("head")
    core = s % 2
    other = 1 - core
    x = (s // 2) % 2
    z = s // 4
    sibling = s + 1 - 2 * core
    partner = s + 2 - 4 * x
    diagonal = partner + 1 - 2 * core

    def z_peer(e):
        return ((z + e) % NZ) * 4 + s % 4

    def seq_dev(t):
        return (t, k)

    def row_dev(e):
        return (s, k - k % 4 + (k + e) % 4)

    k_far = (k + 4) % NK
    far_dev = (s, k_far)

    def weight_dev(e):
        kk = (k + e) % NK
        diff = (kk // 4 - k // 4) * (kk // 4 - k // 4)
        return (s + diff * (2 - 4 * x), kk)

    barrier = pltpu.get_barrier_semaphore()
    targets = [seq_dev(sibling), seq_dev(partner), seq_dev(diagonal)]
    targets += [seq_dev(z_peer(e)) for e in (1, NZ - 1)]
    targets += [row_dev(e) for e in range(1, 4)] + [far_dev]
    targets += [weight_dev(e) for e in range(1, NK)]
    for t in targets:
        pl.semaphore_signal(barrier, inc=1, device_id=t, device_id_type=MESH)

    def local(src, dst, n):
        copy = pltpu.make_async_copy(src, dst, local_sem.at[n])
        copy.start()
        return copy

    loads = [
        local(src, dst, n)
        for n, (src, dst) in enumerate((
            (k_hbm, k_in), (v_hbm, v_in), (q_hbm, q_in),
            (order_hbm, order), (lengths_hbm, lengths), (w_hbm, wfull), (og_hbm, og),
        ))
    ]

    own_cols = pl.ds(pl.multiple_of(core * HD, HD), HD)
    other_cols = pl.ds(pl.multiple_of(other * HD, HD), HD)
    xk, xv, xq, xg = (xa.at[a] for a in (KEYS, VALUES, QUERIES, GRADS))
    half_rows = (pl.multiple_of(core * HALF, HALF), pl.multiple_of(other * HALF, HALF))

    def rows_of(block, j):
        return pl.ds(pl.multiple_of(block * BLK + half_rows[j], HALF), HALF)

    own_rows = rows_of(1, 0)
    for c in loads[:3]:
        c.wait()
    xk[own_rows, :] = k_in[:, own_cols]
    xv[own_rows, :] = v_in[:, own_cols]
    xq[own_rows, :] = q_in[:, own_cols]
    pl.semaphore_wait(barrier, len(targets))

    counter = [0]
    pending = []

    def plan(src, dst, target):
        n = counter[0]
        counter[0] += 1
        copy = pltpu.make_async_remote_copy(
            src_ref=src, dst_ref=dst, send_sem=send_sem.at[n], recv_sem=recv_sem.at[n],
            device_id=target, device_id_type=MESH,
        )
        pending.append(copy)
        return copy

    def remote(src, dst, target):
        copy = plan(src, dst, target)
        copy.start()
        return copy

    def ring_copy(a, back, t, j):
        src, dst = (1 + (9 - t) % NZ, 9 - t) if back else (t, 1 + t)
        return pltpu.make_async_remote_copy(
            src_ref=xa.at[a, rows_of(src, j), :], dst_ref=xa.at[a, rows_of(dst, j), :],
            send_sem=ring_send_sem.at[a, back, t - 1, j],
            recv_sem=ring_recv_sem.at[a, back, t - 1, j],
            device_id=seq_dev(z_peer(NZ - 1 if back else 1)), device_id_type=MESH,
        )

    def ring_start(a, j):
        for back in (0, 1):
            ring_copy(a, back, 1, j).start()

    def ring_service(a, t):
        for j in (0, 1):
            for back in (0, 1):
                if j == back:
                    ring_copy(a, back, t, j).wait_recv()

                    @pl.when(t < 4)
                    def _():
                        ring_copy(a, back, t + 1, j).start()
                else:
                    @pl.when(t < 4)
                    def _():
                        ring_copy(a, back, t, j).wait_recv()

                    @pl.when(t < 3)
                    def _():
                        ring_copy(a, back, t + 1, j).start()

    def to_sibling(src, arr):
        return remote(src.at[:, other_cols], arr.at[rows_of(1, 0), :], seq_dev(sibling))

    def to_pair(src, arr):
        return (
            remote(src.at[:, own_cols], arr.at[rows_of(0, 0), :], seq_dev(partner)),
            remote(src.at[:, other_cols], arr.at[rows_of(0, 0), :], seq_dev(diagonal)),
        )

    sib_k = to_sibling(k_in, xk)
    sib_v = to_sibling(v_in, xv)
    ring_start(KEYS, 0)
    ring_start(VALUES, 0)
    sib_q = to_sibling(q_in, xq)
    pair_q = to_pair(q_in, xq)
    sib_k.wait_recv()
    ring_start(KEYS, 1)
    sib_v.wait_recv()
    ring_start(VALUES, 1)

    for c in loads[5:]:
        c.wait()
    da_acc[...] = jnp.zeros((HALF, HALF), F32)

    def da_body(i, _):
        cols = pl.ds(pl.multiple_of(i * 1024, 1024), 1024)
        da_acc[...] += dot_nt(og[:, cols], wfull[:, cols])
        return 0

    lax.fori_loop(0, 4, da_body, 0)
    da[...] = da_acc[...].astype(BF16)
    xg[own_rows, :] = da[:, own_cols]
    sib_g = to_sibling(da, xg)
    pair_g = to_pair(da, xg)
    pair_k = to_pair(k_in, xk)
    pair_v = to_pair(v_in, xv)

    for c in loads[3:5]:
        c.wait()
    ends = []
    total = jnp.int32(0)
    for j in range(DOCS):
        total = total + lengths[j]
        ends.append(total)

    def chip_group(zz, xx):
        return zz * 8 + xx * 4

    lane = lax.broadcasted_iota(jnp.int32, (GROUP, GROUP), 1)
    sub = lax.broadcasted_iota(jnp.int32, (GROUP, GROUP), 0)

    def place_body(g, _):
        xx = jnp.where(g < 4, 1 - x, x)
        pos = order[chip_group(z, xx) + g % 4] * GROUP + sub
        low = jnp.zeros((GROUP, GROUP), jnp.int32)
        high = jnp.full((GROUP, GROUP), 1 << 29, jnp.int32)
        for e in ends:
            low = jnp.maximum(low, jnp.where(pos >= e, e, 0))
            high = jnp.minimum(high, jnp.where(pos < e, e, 1 << 29))
        rows = pl.ds(pl.multiple_of(g * GROUP, GROUP), GROUP)
        first[rows, :] = low - lane
        place[rows, :] = pos - lane
        last[rows, :] = high - 1 - lane
        return 0

    lax.fori_loop(0, 8, place_body, 0)

    def base(d, j):
        return order[chip_group((z + NZ - d) % NZ, x) + j] * GROUP

    m_acc[...] = jnp.full((PAIR, HD), LOWEST, F32)
    for acc in (l_acc, o_acc, a1_acc, a2_acc, dk_acc, dv_acc):
        acc[...] = jnp.zeros((PAIR, HD), F32)

    ring_service(KEYS, 1)

    col_half = pl.ds(pl.multiple_of(core * 256, 256), 256)
    w_copies = []
    for e in range(1, NK):
        kk = (k + e) % NK
        src = wfull.at[:, pl.ds(pl.multiple_of(kk * 512 + core * 256, 256), 256)]
        w_copies.append(remote(src, wg.at[k, :, col_half], weight_dev(e)))
    wg[k, :, :] = wfull[:, pl.ds(pl.multiple_of(k * 512, 512), 512)]
    w_sib = []
    for e in range(1, NK):
        ref = wg.at[(k + NK - e) % NK, :, col_half]
        w_sib.append(plan(ref, ref, seq_dev(sibling)))

    copy_l = plan(st_send.at[0], st_recv, seq_dev(partner))
    copy_o = plan(o_send, o_recv, seq_dev(partner))
    att_far = plan(attg.at[k], attg.at[k], far_dev)
    att_near = [plan(attg.at[k], attg.at[k], row_dev(e)) for e in range(1, 4)]
    att_relay = [plan(attg.at[k_far], attg.at[k_far], row_dev(e)) for e in range(1, 4)]
    grads = [
        [
            plan(grad_send.at[n, m], grad_recv.at[n, m], seq_dev(t))
            for m, t in enumerate((sibling, partner, diagonal))
        ]
        for n in range(3)
    ]

    def block_rows(d):
        return pl.ds(pl.multiple_of((1 + d) * BLK, BLK), BLK)

    def block_of(i):
        return jnp.where(i % 2 == 1, (i + 1) // 2, (NZ - i // 2) % NZ)

    own, theirs = pl.ds(BLK, BLK), pl.ds(0, BLK)

    def forward(blocks, rows):
        q, grad = xq[rows, :], xg[rows, :]
        low, high = first[rows, :], place[rows, :]
        parts, dprobs = [], []
        for d in blocks:
            logits = dot_nt(q, xk[block_rows(d), :])
            dprobs.append(dot_nt(grad, xv[block_rows(d), :]))
            for j in range(4):
                b = base(d, j)
                part = logits[:, j * GROUP:(j + 1) * GROUP] * SCALE2
                parts.append(jnp.where((low <= b) & (high >= b), part, HIDDEN))
        top = functools.reduce(jnp.maximum, parts)
        old = m_acc[rows, :]
        new = jnp.maximum(old, jnp.max(top, axis=1, keepdims=True))
        factor = jnp.exp2(old - new)
        weights = [jnp.exp2(part - new) for part in parts]
        l_acc[rows, :] = l_acc[rows, :] * factor + functools.reduce(jnp.add, weights)
        m_acc[rows, :] = new
        o_sum = o_acc[rows, :] * factor
        a1_sum = a1_acc[rows, :] * factor
        a2_sum = a2_acc[rows, :] * factor
        for n, d in enumerate(blocks):
            key = xk[block_rows(d), :]
            mine = weights[4 * n:4 * n + 4]
            both = dot_nn(
                jnp.concatenate([w.astype(BF16) for w in mine], axis=1),
                jnp.concatenate([xv[block_rows(d), :], key], axis=1),
            )
            o_sum = o_sum + both[:, :HD]
            a2_sum = a2_sum + both[:, HD:]
            scores = [
                (w * dprobs[n][:, j * GROUP:(j + 1) * GROUP]).astype(BF16)
                for j, w in enumerate(mine)
            ]
            a1_sum = a1_sum + dot_nn(jnp.concatenate(scores, axis=1), key)
        o_acc[rows, :] = o_sum
        a1_acc[rows, :] = a1_sum
        a2_acc[rows, :] = a2_sum

    def close(rows):
        totals = jnp.maximum(jnp.sum(l_acc[rows, :], axis=1, keepdims=True), 1e-30)
        totals = jnp.broadcast_to(totals, (BLK, HD))
        return o_acc[rows, :] / totals, m_acc[rows, :] + jnp.log(totals) * LOG2E

    ring_service(VALUES, 1)
    for c in (sib_q, sib_g) + pair_q + pair_g:
        c.wait_recv()

    def forward_step(n, _):
        @pl.when((n % 2 == 0) & (n >= 4))
        def _():
            ring_service((n // 2) % 2, n // 4 + 1)

        @pl.when(n == 10)
        def _():
            for a in (QUERIES, GRADS):
                for j in (0, 1):
                    ring_start(a, j)

        @pl.when(n == 15)
        def _():
            o_part, lse_part = close(theirs)
            o_send[...] = o_part.astype(BF16)
            st_send[0, :, :] = lse_part.T[0:8, :]
            copy_l.start()
            copy_o.start()

        forward((block_of(n // 2),), pl.ds(pl.multiple_of((n % 2) * BLK, BLK), BLK))
        return 0

    lax.fori_loop(0, 16, forward_step, 0)
    ring_service(QUERIES, 1)
    o_own, lse_own = close(own)
    ring_service(GRADS, 1)
    copy_l.wait_recv()
    copy_o.wait_recv()

    def to_col(row):
        return jnp.broadcast_to(row, (HD, BLK)).T

    lse_other = to_col(st_recv[0:1, :])
    top = jnp.maximum(lse_own, lse_other)
    lse = top + jnp.log(jnp.exp2(lse_own - top) + jnp.exp2(lse_other - top)) * LOG2E
    merged = o_own * jnp.exp2(lse_own - lse) + o_recv[...].astype(F32) * jnp.exp2(lse_other - lse)
    attention = merged.astype(BF16)
    att[...] = attention
    delta = jnp.sum(
        attention.astype(F32) * xg[block_rows(0), :].astype(F32), axis=1, keepdims=True
    )
    delta = jnp.broadcast_to(delta, (BLK, HD))
    row8 = lax.broadcasted_iota(jnp.int32, (8, BLK), 0)
    st_z[0, :, :] = jnp.where(row8 == 0, lse.T[0:8, :], delta.T[0:8, :])
    def stats_copy(back, t):
        src, dst = ((9 - t) % NZ, NZ - t) if back else (t - 1, t)
        return pltpu.make_async_remote_copy(
            src_ref=st_z.at[src], dst_ref=st_z.at[dst],
            send_sem=stat_send_sem.at[back, t - 1], recv_sem=stat_recv_sem.at[back, t - 1],
            device_id=seq_dev(z_peer(NZ - 1 if back else 1)), device_id_type=MESH,
        )

    def stats_service(t):
        stats_copy(0, t).wait_recv()
        stats_copy(0, t + 1).start()
        stats_copy(1, t).wait_recv()

        @pl.when(t < 3)
        def _():
            stats_copy(1, t + 1).start()

    for back in (0, 1):
        stats_copy(back, 1).start()
    copy_sp = remote(st_z.at[0], st_par, seq_dev(partner))
    copy_a = remote(
        att.at[pl.ds(half_rows[1], HALF), :], attg.at[k, :, own_cols], seq_dev(sibling)
    )
    attg[k, :, own_cols] = att[pl.ds(half_rows[0], HALF), :]

    def close_queries(rows, lse_rows, delta_rows):
        factor = jnp.exp2(m_acc[rows, :] - lse_rows) * SCALE
        dq_acc[rows, :] = (a1_acc[rows, :] - delta_rows * a2_acc[rows, :]) * factor

    def key_side(blocks, keys):
        low, high = place[keys, :], last[keys, :]
        key, value = xk[keys, :], xv[keys, :]
        dk, dv = dk_acc[keys, :], dv_acc[keys, :]
        for d in blocks:
            query, grad = xq[block_rows(d), :], xg[block_rows(d), :]
            logits = dot_nt(key, query)
            dprobs = dot_nt(value, grad)
            probs, scores = [], []
            for j in range(4):
                b = base(d, j)
                cols = slice(j * GROUP, (j + 1) * GROUP)
                log_t = st_z[d, 0:1, cols]
                dlt = st_z[d, 1:2, cols]
                part = jnp.where(
                    (low <= b) & (high >= b), logits[:, cols] * SCALE2 - log_t, HIDDEN
                )
                prob = jnp.exp2(part)
                probs.append(prob.astype(BF16))
                scores.append((prob * (dprobs[:, cols] - dlt)).astype(BF16))
            dv = dv + dot_nn(jnp.concatenate(probs, axis=1), grad)
            dk = dk + dot_nn(jnp.concatenate(scores, axis=1), query)
        dk_acc[keys, :] = dk
        dv_acc[keys, :] = dv

    def send_grad(n, acc, scale, m):
        block, j = ((1, 1), (0, 0), (0, 1))[m]
        grad_send[n, m, :, :] = (acc[rows_of(block, j), :] * scale).astype(BF16)
        grads[n][m].start()

    def finish_grad(n, acc, scale, out):
        for c in grads[n]:
            c.wait_recv()
        mine = acc[rows_of(1, 0), :] * scale + grad_recv[n, 1, :, :].astype(F32)
        not_mine = grad_recv[n, 0, :, :].astype(F32) + grad_recv[n, 2, :, :].astype(F32)
        grad_out[n, :, own_cols] = mine.astype(BF16)
        grad_out[n, :, other_cols] = not_mine.astype(BF16)
        return local(grad_out.at[n], out, 7 + n)

    close_queries(own, lse, delta)
    for c in pair_k + pair_v:
        c.wait_recv()

    def key_step(i, _):
        @pl.when((i == 1) | (i == 4))
        def _():
            ring_service(QUERIES, i // 3 + 2)

        @pl.when((i == 2) | (i == 5))
        def _():
            ring_service(GRADS, i // 3 + 2)

        @pl.when(i == 6)
        def _():
            ring_service(QUERIES, 4)

        @pl.when(i % 2 == 1)
        def _():
            stats_service((i + 1) // 2)

        @pl.when(i == 1)
        def _():
            copy_a.wait_recv()
            for c in [att_far] + att_near:
                c.start()

        @pl.when(i == 2)
        def _():
            copy_sp.wait_recv()
            close_queries(theirs, to_col(st_par[0:1, :]), to_col(st_par[1:2, :]))
            for m in (1, 2, 0):
                send_grad(0, dq_acc, 1.0, m)

        @pl.when(i == 3)
        def _():
            for c, d in zip(w_copies, w_sib):
                c.wait_recv()
                d.start()

        @pl.when(i == 5)
        def _():
            att_far.wait_recv()
            for c in att_relay:
                c.start()

        key_side((block_of(i),), pl.ds(0, PAIR))
        return 0

    lax.fori_loop(0, 7, key_step, 0)
    ring_service(GRADS, 4)
    stats_copy(0, 4).wait_recv()

    def last_step(i, _):
        @pl.when(i == 1)
        def _():
            for m in (1, 2):
                send_grad(2, dv_acc, 1.0, m)
                send_grad(1, dk_acc, SCALE, m)

        key_side((4,), pl.ds(pl.multiple_of(i * BLK, BLK), BLK))
        return 0

    lax.fori_loop(0, 2, last_step, 0)
    send_grad(2, dv_acc, 1.0, 0)
    send_grad(1, dk_acc, SCALE, 0)
    stores = [finish_grad(0, dq_acc, 1.0, dq_hbm)]

    for c in att_near + att_relay + w_sib:
        c.wait_recv()

    def project(i, total):
        return total + dot_nn(attg[i, :, :], wg[i, :, :])

    layer_out[...] = lax.fori_loop(0, NK, project, jnp.zeros((HALF, 512), F32)).astype(BF16)
    stores.append(local(layer_out, layer_hbm, 10))
    stores.append(finish_grad(2, dv_acc, 1.0, dv_hbm))
    stores.append(finish_grad(1, dk_acc, SCALE, dk_hbm))
    for c in stores:
        c.wait()
    for c in pending:
        c.wait_send()
    for t in range(1, 5):
        stats_copy(0, t).wait_send()
    for t in range(1, 4):
        stats_copy(1, t).wait_send()

    def drain(a, _):
        for j in (0, 1):
            for back in (0, 1):
                for t in range(1, 5 if j == back else 4):
                    ring_copy(a, back, t, j).wait_send()
        return 0

    lax.fori_loop(0, 4, drain, 0)


COPIES = 56
VMEM_BYTES = 62 * 1024 * 1024


def emit(a, b, c, d, a_out, b_out, c_out, d_out, a_buf, b_buf, c_buf, d_buf, sem):
    steps = ((a, a_buf, a_out), (b, b_buf, b_out), (c, c_buf, c_out), (d, d_buf, d_out))
    loads = [pltpu.make_async_copy(t[0], t[1], sem.at[0, n]) for n, t in enumerate(steps)]
    stores = [pltpu.make_async_copy(t[1], t[2], sem.at[1, n]) for n, t in enumerate(steps)]
    for copy in loads:
        copy.start()
    for load, store in zip(loads, stores):
        load.wait()
        store.start()
    for copy in stores:
        copy.wait()


def per_device(queries, key_vectors, value_vectors, group_order, doc_lengths, out_grad, out_weight):
    hbm = pl.BlockSpec(memory_space=pl.ANY)
    local = pltpu.VMEM((HALF, 2 * HD), BF16)
    pair_f32 = pltpu.VMEM((PAIR, HD), F32)
    pair_int = pltpu.VMEM((PAIR, HD), jnp.int32)
    results = pl.pallas_call(
        kernel,
        out_shape=(
            jax.ShapeDtypeStruct((HALF, 512), BF16),
            jax.ShapeDtypeStruct((HALF, 2 * HD), BF16),
            jax.ShapeDtypeStruct((HALF, 2 * HD), BF16),
            jax.ShapeDtypeStruct((HALF, 2 * HD), BF16),
        ),
        in_specs=[hbm] * 7,
        out_specs=(hbm, hbm, hbm, hbm),
        scratch_shapes=[
            pltpu.SMEM((64,), jnp.int32),
            pltpu.SMEM((DOCS,), jnp.int32),
            local, local, local,
            pltpu.VMEM((HALF, 512), BF16),
            pltpu.VMEM((3, HALF, 2 * HD), BF16),
            pltpu.VMEM((4, 9 * BLK, HD), BF16),
            pltpu.VMEM((HALF, 4096), BF16),
            pltpu.VMEM((HALF, 4096), BF16),
            pltpu.VMEM((NK, HALF, 512), BF16),
            pltpu.VMEM((HALF, HALF), BF16),
            pltpu.VMEM((HALF, HALF), F32),
            pltpu.VMEM((BLK, HD), BF16),
            pltpu.VMEM((NK, HALF, HALF), BF16),
            pair_int, pair_int, pair_int,
            pair_f32, pair_f32, pair_f32, pair_f32, pair_f32, pair_f32, pair_f32, pair_f32,
            pltpu.VMEM((BLK, HD), BF16),
            pltpu.VMEM((BLK, HD), BF16),
            pltpu.VMEM((1, 8, BLK), F32),
            pltpu.VMEM((8, BLK), F32),
            pltpu.VMEM((NZ, 8, BLK), F32),
            pltpu.VMEM((8, BLK), F32),
            pltpu.VMEM((3, 3, HALF, HD), BF16),
            pltpu.VMEM((3, 3, HALF, HD), BF16),
            pltpu.SemaphoreType.DMA((COPIES,)),
            pltpu.SemaphoreType.DMA((COPIES,)),
            pltpu.SemaphoreType.DMA((4, 2, 4, 2)),
            pltpu.SemaphoreType.DMA((4, 2, 4, 2)),
            pltpu.SemaphoreType.DMA((2, 4)),
            pltpu.SemaphoreType.DMA((2, 4)),
            pltpu.SemaphoreType.DMA((11,)),
        ],
        compiler_params=pltpu.CompilerParams(
            collective_id=0, has_side_effects=True, vmem_limit_bytes=VMEM_BYTES
        ),
        name="attention_grads",
    )(group_order, doc_lengths, queries, key_vectors, value_vectors, out_grad, out_weight)
    return pl.pallas_call(
        emit,
        out_shape=tuple(jax.ShapeDtypeStruct(r.shape, r.dtype) for r in results),
        in_specs=[pl.BlockSpec(memory_space=pl.ANY)] * 4,
        out_specs=(pl.BlockSpec(memory_space=pl.ANY),) * 4,
        scratch_shapes=[pltpu.VMEM(r.shape, r.dtype) for r in results]
        + [pltpu.SemaphoreType.DMA((2, 4))],
        compiler_params=pltpu.CompilerParams(vmem_limit_bytes=VMEM_BYTES),
        name="emit",
    )(*results)


def solution(mesh):
    return jax.shard_map(
        per_device,
        mesh=mesh,
        in_specs=(
            P("seq", "head"),
            P("seq", "head"),
            P("seq", "head"),
            P(),
            P(),
            P("seq", None),
            P("head", None),
        ),
        out_specs=(P("seq", "head"), P("seq", "head"), P("seq", "head"), P("seq", "head")),
        check_vma=False,
    )
```

```python
import functools
import math

import jax
import jax.numpy as jnp
from jax import lax
from jax.experimental import pallas as pl
from jax.experimental.pallas import tpu as pltpu
from jax.sharding import PartitionSpec as P

HD = 128
GROUP = 128
DOCS = 8
NZ = 8
NK = 8
BLK = 512
HALF = 256
PAIR = 2 * BLK
KEYS, VALUES, QUERIES, GRADS = range(4)
LOG2E = math.log2(math.e)
SCALE = 1.0 / math.sqrt(HD)
SCALE2 = SCALE * LOG2E
HIDDEN = -1e30
LOWEST = -5e29
F32 = jnp.float32
BF16 = jnp.bfloat16
MESH = pl.DeviceIdType.MESH


def dot_nt(a, b):
    return lax.dot_general(a, b, (((1,), (1,)), ((), ())), preferred_element_type=F32)


def dot_nn(a, b):
    return jnp.dot(a, b, preferred_element_type=F32)


def kernel(
    order_hbm, lengths_hbm, q_hbm, k_hbm, v_hbm, og_hbm, w_hbm,
    layer_hbm, dq_hbm, dk_hbm, dv_hbm,
    order, lengths, q_in, k_in, v_in, layer_out, grad_out,
    xa,
    og, wfull, wg, da, da_acc, att, attg,
    first, place, last,
    o_acc, m_acc, l_acc, a1_acc, a2_acc, dq_acc, dk_acc, dv_acc,
    o_send, o_recv, st_send, st_recv, st_z, st_par, grad_send, grad_recv,
    send_sem, recv_sem, ring_send_sem, ring_recv_sem, stat_send_sem, stat_recv_sem, local_sem,
):
    s = lax.axis_index("seq")
    k = lax.axis_index("head")
    core = s % 2
    other = 1 - core
    x = (s // 2) % 2
    z = s // 4
    sibling = s + 1 - 2 * core
    partner = s + 2 - 4 * x
    diagonal = partner + 1 - 2 * core

    def z_peer(e):
        return ((z + e) % NZ) * 4 + s % 4

    def seq_dev(t):
        return (t, k)

    def row_dev(e):
        return (s, k - k % 4 + (k + e) % 4)

    k_far = (k + 4) % NK
    far_dev = (s, k_far)

    def weight_dev(e):
        kk = (k + e) % NK
        diff = (kk // 4 - k // 4) * (kk // 4 - k // 4)
        return (s + diff * (2 - 4 * x), kk)

    barrier = pltpu.get_barrier_semaphore()
    targets = [seq_dev(sibling), seq_dev(partner), seq_dev(diagonal)]
    targets += [seq_dev(z_peer(e)) for e in (1, NZ - 1)]
    targets += [row_dev(e) for e in range(1, 4)] + [far_dev]
    targets += [weight_dev(e) for e in range(1, NK)]
    for t in targets:
        pl.semaphore_signal(barrier, inc=1, device_id=t, device_id_type=MESH)

    def local(src, dst, n):
        copy = pltpu.make_async_copy(src, dst, local_sem.at[n])
        copy.start()
        return copy

    loads = [
        local(src, dst, n)
        for n, (src, dst) in enumerate((
            (k_hbm, k_in), (v_hbm, v_in), (q_hbm, q_in),
            (order_hbm, order), (lengths_hbm, lengths), (w_hbm, wfull), (og_hbm, og),
        ))
    ]

    own_cols = pl.ds(pl.multiple_of(core * HD, HD), HD)
    other_cols = pl.ds(pl.multiple_of(other * HD, HD), HD)
    xk, xv, xq, xg = (xa.at[a] for a in (KEYS, VALUES, QUERIES, GRADS))
    half_rows = (pl.multiple_of(core * HALF, HALF), pl.multiple_of(other * HALF, HALF))

    def rows_of(block, j):
        return pl.ds(pl.multiple_of(block * BLK + half_rows[j], HALF), HALF)

    own_rows = rows_of(1, 0)
    for c in loads[:3]:
        c.wait()
    xk[own_rows, :] = k_in[:, own_cols]
    xv[own_rows, :] = v_in[:, own_cols]
    xq[own_rows, :] = q_in[:, own_cols]
    pl.semaphore_wait(barrier, len(targets))

    counter = [0]
    pending = []

    def plan(src, dst, target):
        n = counter[0]
        counter[0] += 1
        copy = pltpu.make_async_remote_copy(
            src_ref=src, dst_ref=dst, send_sem=send_sem.at[n], recv_sem=recv_sem.at[n],
            device_id=target, device_id_type=MESH,
        )
        pending.append(copy)
        return copy

    def remote(src, dst, target):
        copy = plan(src, dst, target)
        copy.start()
        return copy

    def ring_copy(a, back, t, j):
        src, dst = (1 + (9 - t) % NZ, 9 - t) if back else (t, 1 + t)
        return pltpu.make_async_remote_copy(
            src_ref=xa.at[a, rows_of(src, j), :], dst_ref=xa.at[a, rows_of(dst, j), :],
            send_sem=ring_send_sem.at[a, back, t - 1, j],
            recv_sem=ring_recv_sem.at[a, back, t - 1, j],
            device_id=seq_dev(z_peer(NZ - 1 if back else 1)), device_id_type=MESH,
        )

    def ring_start(a, j):
        for back in (0, 1):
            ring_copy(a, back, 1, j).start()

    def ring_service(a, t):
        for j in (0, 1):
            for back in (0, 1):
                if j == back:
                    ring_copy(a, back, t, j).wait_recv()

                    @pl.when(t < 4)
                    def _():
                        ring_copy(a, back, t + 1, j).start()
                else:
                    @pl.when(t < 4)
                    def _():
                        ring_copy(a, back, t, j).wait_recv()

                    @pl.when(t < 3)
                    def _():
                        ring_copy(a, back, t + 1, j).start()

    def to_sibling(src, arr):
        return remote(src.at[:, other_cols], arr.at[rows_of(1, 0), :], seq_dev(sibling))

    def to_pair(src, arr):
        return (
            remote(src.at[:, own_cols], arr.at[rows_of(0, 0), :], seq_dev(partner)),
            remote(src.at[:, other_cols], arr.at[rows_of(0, 0), :], seq_dev(diagonal)),
        )

    ring_start(KEYS, 0)
    sib_k = to_sibling(k_in, xk)
    sib_v = to_sibling(v_in, xv)
    ring_start(VALUES, 0)
    sib_q = to_sibling(q_in, xq)
    pair_q = to_pair(q_in, xq)
    sib_k.wait_recv()
    ring_start(KEYS, 1)
    sib_v.wait_recv()
    ring_start(VALUES, 1)

    for c in loads[5:]:
        c.wait()
    da_acc[...] = jnp.zeros((HALF, HALF), F32)

    def da_body(i, _):
        cols = pl.ds(pl.multiple_of(i * 1024, 1024), 1024)
        da_acc[...] += dot_nt(og[:, cols], wfull[:, cols])
        return 0

    lax.fori_loop(0, 4, da_body, 0)
    da[...] = da_acc[...].astype(BF16)
    xg[own_rows, :] = da[:, own_cols]
    sib_g = to_sibling(da, xg)
    pair_g = to_pair(da, xg)
    pair_k = to_pair(k_in, xk)
    pair_v = to_pair(v_in, xv)

    for c in loads[3:5]:
        c.wait()
    ends = []
    total = jnp.int32(0)
    for j in range(DOCS):
        total = total + lengths[j]
        ends.append(total)

    def chip_group(zz, xx):
        return zz * 8 + xx * 4

    lane = lax.broadcasted_iota(jnp.int32, (GROUP, GROUP), 1)
    sub = lax.broadcasted_iota(jnp.int32, (GROUP, GROUP), 0)

    def place_body(g, _):
        xx = jnp.where(g < 4, 1 - x, x)
        pos = order[chip_group(z, xx) + g % 4] * GROUP + sub
        low = jnp.zeros((GROUP, GROUP), jnp.int32)
        high = jnp.full((GROUP, GROUP), 1 << 29, jnp.int32)
        for e in ends:
            low = jnp.maximum(low, jnp.where(pos >= e, e, 0))
            high = jnp.minimum(high, jnp.where(pos < e, e, 1 << 29))
        rows = pl.ds(pl.multiple_of(g * GROUP, GROUP), GROUP)
        first[rows, :] = low - lane
        place[rows, :] = pos - lane
        last[rows, :] = high - 1 - lane
        return 0

    lax.fori_loop(0, 8, place_body, 0)

    def base(d, j):
        return order[chip_group((z + NZ - d) % NZ, x) + j] * GROUP

    m_acc[...] = jnp.full((PAIR, HD), LOWEST, F32)
    for acc in (l_acc, o_acc, a1_acc, a2_acc, dk_acc, dv_acc):
        acc[...] = jnp.zeros((PAIR, HD), F32)

    ring_service(KEYS, 1)

    col_half = pl.ds(pl.multiple_of(core * 256, 256), 256)
    w_copies = []
    for e in range(1, NK):
        kk = (k + e) % NK
        src = wfull.at[:, pl.ds(pl.multiple_of(kk * 512 + core * 256, 256), 256)]
        w_copies.append(remote(src, wg.at[k, :, col_half], weight_dev(e)))
    wg[k, :, :] = wfull[:, pl.ds(pl.multiple_of(k * 512, 512), 512)]
    w_sib = []
    for e in range(1, NK):
        ref = wg.at[(k + NK - e) % NK, :, col_half]
        w_sib.append(plan(ref, ref, seq_dev(sibling)))

    copy_l = plan(st_send.at[0], st_recv, seq_dev(partner))
    copy_o = plan(o_send, o_recv, seq_dev(partner))
    att_far = plan(attg.at[k], attg.at[k], far_dev)
    att_near = [plan(attg.at[k], attg.at[k], row_dev(e)) for e in range(1, 4)]
    att_relay = [plan(attg.at[k_far], attg.at[k_far], row_dev(e)) for e in range(1, 4)]
    grads = [
        [
            plan(grad_send.at[n, m], grad_recv.at[n, m], seq_dev(t))
            for m, t in enumerate((sibling, partner, diagonal))
        ]
        for n in range(3)
    ]

    def block_rows(d):
        return pl.ds(pl.multiple_of((1 + d) * BLK, BLK), BLK)

    def block_of(i):
        return jnp.where(i % 2 == 1, (i + 1) // 2, (NZ - i // 2) % NZ)

    own, theirs = pl.ds(BLK, BLK), pl.ds(0, BLK)

    def forward(blocks, rows):
        q, grad = xq[rows, :], xg[rows, :]
        low, high = first[rows, :], place[rows, :]
        parts, dprobs = [], []
        for d in blocks:
            logits = dot_nt(q, xk[block_rows(d), :])
            dprobs.append(dot_nt(grad, xv[block_rows(d), :]))
            for j in range(4):
                b = base(d, j)
                part = logits[:, j * GROUP:(j + 1) * GROUP] * SCALE2
                parts.append(jnp.where((low <= b) & (high >= b), part, HIDDEN))
        top = functools.reduce(jnp.maximum, parts)
        old = m_acc[rows, :]
        new = jnp.maximum(old, jnp.max(top, axis=1, keepdims=True))
        factor = jnp.exp2(old - new)
        weights = [jnp.exp2(part - new) for part in parts]
        l_acc[rows, :] = l_acc[rows, :] * factor + functools.reduce(jnp.add, weights)
        m_acc[rows, :] = new
        o_sum = o_acc[rows, :] * factor
        a1_sum = a1_acc[rows, :] * factor
        a2_sum = a2_acc[rows, :] * factor
        for n, d in enumerate(blocks):
            key = xk[block_rows(d), :]
            mine = weights[4 * n:4 * n + 4]
            both = dot_nn(
                jnp.concatenate([w.astype(BF16) for w in mine], axis=1),
                jnp.concatenate([xv[block_rows(d), :], key], axis=1),
            )
            o_sum = o_sum + both[:, :HD]
            a2_sum = a2_sum + both[:, HD:]
            scores = [
                (w * dprobs[n][:, j * GROUP:(j + 1) * GROUP]).astype(BF16)
                for j, w in enumerate(mine)
            ]
            a1_sum = a1_sum + dot_nn(jnp.concatenate(scores, axis=1), key)
        o_acc[rows, :] = o_sum
        a1_acc[rows, :] = a1_sum
        a2_acc[rows, :] = a2_sum

    def close(rows):
        totals = jnp.maximum(jnp.sum(l_acc[rows, :], axis=1, keepdims=True), 1e-30)
        totals = jnp.broadcast_to(totals, (BLK, HD))
        return o_acc[rows, :] / totals, m_acc[rows, :] + jnp.log(totals) * LOG2E

    ring_service(VALUES, 1)
    for c in (sib_q, sib_g) + pair_q + pair_g:
        c.wait_recv()

    def forward_step(n, _):
        @pl.when((n % 2 == 0) & (n >= 4))
        def _():
            ring_service((n // 2) % 2, n // 4 + 1)

        @pl.when(n == 8)
        def _():
            ring_start(QUERIES, 0)

        @pl.when(n == 10)
        def _():
            ring_start(QUERIES, 1)
            for j in (0, 1):
                ring_start(GRADS, j)

        @pl.when(n == 15)
        def _():
            o_part, lse_part = close(theirs)
            o_send[...] = o_part.astype(BF16)
            st_send[0, :, :] = lse_part.T[0:8, :]
            copy_l.start()
            copy_o.start()

        forward((block_of(n // 2),), pl.ds(pl.multiple_of((n % 2) * BLK, BLK), BLK))
        return 0

    lax.fori_loop(0, 16, forward_step, 0)
    ring_service(QUERIES, 1)
    o_own, lse_own = close(own)
    ring_service(GRADS, 1)
    copy_l.wait_recv()
    copy_o.wait_recv()

    def to_col(row):
        return jnp.broadcast_to(row, (HD, BLK)).T

    lse_other = to_col(st_recv[0:1, :])
    top = jnp.maximum(lse_own, lse_other)
    lse = top + jnp.log(jnp.exp2(lse_own - top) + jnp.exp2(lse_other - top)) * LOG2E
    merged = o_own * jnp.exp2(lse_own - lse) + o_recv[...].astype(F32) * jnp.exp2(lse_other - lse)
    attention = merged.astype(BF16)
    att[...] = attention
    delta = jnp.sum(
        attention.astype(F32) * xg[block_rows(0), :].astype(F32), axis=1, keepdims=True
    )
    delta = jnp.broadcast_to(delta, (BLK, HD))
    row8 = lax.broadcasted_iota(jnp.int32, (8, BLK), 0)
    st_z[0, :, :] = jnp.where(row8 == 0, lse.T[0:8, :], delta.T[0:8, :])
    def stats_copy(back, t):
        src, dst = ((9 - t) % NZ, NZ - t) if back else (t - 1, t)
        return pltpu.make_async_remote_copy(
            src_ref=st_z.at[src], dst_ref=st_z.at[dst],
            send_sem=stat_send_sem.at[back, t - 1], recv_sem=stat_recv_sem.at[back, t - 1],
            device_id=seq_dev(z_peer(NZ - 1 if back else 1)), device_id_type=MESH,
        )

    def stats_service(t):
        stats_copy(0, t).wait_recv()
        stats_copy(0, t + 1).start()
        stats_copy(1, t).wait_recv()

        @pl.when(t < 3)
        def _():
            stats_copy(1, t + 1).start()

    for back in (0, 1):
        stats_copy(back, 1).start()
    copy_sp = remote(st_z.at[0], st_par, seq_dev(partner))
    copy_a = remote(
        att.at[pl.ds(half_rows[1], HALF), :], attg.at[k, :, own_cols], seq_dev(sibling)
    )
    attg[k, :, own_cols] = att[pl.ds(half_rows[0], HALF), :]

    def close_queries(rows, lse_rows, delta_rows):
        factor = jnp.exp2(m_acc[rows, :] - lse_rows) * SCALE
        dq_acc[rows, :] = (a1_acc[rows, :] - delta_rows * a2_acc[rows, :]) * factor

    def key_side(blocks, keys):
        low, high = place[keys, :], last[keys, :]
        key, value = xk[keys, :], xv[keys, :]
        dk, dv = dk_acc[keys, :], dv_acc[keys, :]
        for d in blocks:
            query, grad = xq[block_rows(d), :], xg[block_rows(d), :]
            logits = dot_nt(key, query)
            dprobs = dot_nt(value, grad)
            probs, scores = [], []
            for j in range(4):
                b = base(d, j)
                cols = slice(j * GROUP, (j + 1) * GROUP)
                log_t = st_z[d, 0:1, cols]
                dlt = st_z[d, 1:2, cols]
                part = jnp.where(
                    (low <= b) & (high >= b), logits[:, cols] * SCALE2 - log_t, HIDDEN
                )
                prob = jnp.exp2(part)
                probs.append(prob.astype(BF16))
                scores.append((prob * (dprobs[:, cols] - dlt)).astype(BF16))
            dv = dv + dot_nn(jnp.concatenate(probs, axis=1), grad)
            dk = dk + dot_nn(jnp.concatenate(scores, axis=1), query)
        dk_acc[keys, :] = dk
        dv_acc[keys, :] = dv

    def send_grad(n, acc, scale, m):
        block, j = ((1, 1), (0, 0), (0, 1))[m]
        grad_send[n, m, :, :] = (acc[rows_of(block, j), :] * scale).astype(BF16)
        grads[n][m].start()

    def finish_grad(n, acc, scale, out):
        for c in grads[n]:
            c.wait_recv()
        mine = acc[rows_of(1, 0), :] * scale + grad_recv[n, 1, :, :].astype(F32)
        not_mine = grad_recv[n, 0, :, :].astype(F32) + grad_recv[n, 2, :, :].astype(F32)
        grad_out[n, :, own_cols] = mine.astype(BF16)
        grad_out[n, :, other_cols] = not_mine.astype(BF16)
        return local(grad_out.at[n], out, 7 + n)

    close_queries(own, lse, delta)
    for c in pair_k + pair_v:
        c.wait_recv()

    def key_step(i, _):
        @pl.when((i == 1) | (i == 4))
        def _():
            ring_service(QUERIES, i // 3 + 2)

        @pl.when((i == 2) | (i == 5))
        def _():
            ring_service(GRADS, i // 3 + 2)

        @pl.when(i == 6)
        def _():
            ring_service(QUERIES, 4)

        @pl.when(i % 2 == 1)
        def _():
            stats_service((i + 1) // 2)

        @pl.when(i == 1)
        def _():
            copy_a.wait_recv()
            for c in [att_far] + att_near:
                c.start()

        @pl.when(i == 2)
        def _():
            copy_sp.wait_recv()
            close_queries(theirs, to_col(st_par[0:1, :]), to_col(st_par[1:2, :]))
            for m in (1, 2, 0):
                send_grad(0, dq_acc, 1.0, m)

        @pl.when(i == 3)
        def _():
            for c, d in zip(w_copies, w_sib):
                c.wait_recv()
                d.start()

        @pl.when(i == 5)
        def _():
            att_far.wait_recv()
            for c in att_relay:
                c.start()

        key_side((block_of(i),), pl.ds(0, PAIR))
        return 0

    lax.fori_loop(0, 7, key_step, 0)
    ring_service(GRADS, 4)
    stats_copy(0, 4).wait_recv()

    def last_step(i, _):
        @pl.when(i == 1)
        def _():
            for m in (1, 2):
                send_grad(2, dv_acc, 1.0, m)
                send_grad(1, dk_acc, SCALE, m)

        key_side((4,), pl.ds(pl.multiple_of(i * BLK, BLK), BLK))
        return 0

    lax.fori_loop(0, 2, last_step, 0)
    send_grad(2, dv_acc, 1.0, 0)
    send_grad(1, dk_acc, SCALE, 0)
    stores = [finish_grad(0, dq_acc, 1.0, dq_hbm)]

    for c in att_near + att_relay + w_sib:
        c.wait_recv()

    def project(i, total):
        return total + dot_nn(attg[i, :, :], wg[i, :, :])

    layer_out[...] = lax.fori_loop(0, NK, project, jnp.zeros((HALF, 512), F32)).astype(BF16)
    stores.append(local(layer_out, layer_hbm, 10))
    stores.append(finish_grad(2, dv_acc, 1.0, dv_hbm))
    stores.append(finish_grad(1, dk_acc, SCALE, dk_hbm))
    for c in stores:
        c.wait()
    for c in pending:
        c.wait_send()
    for t in range(1, 5):
        stats_copy(0, t).wait_send()
    for t in range(1, 4):
        stats_copy(1, t).wait_send()

    def drain(a, _):
        for j in (0, 1):
            for back in (0, 1):
                for t in range(1, 5 if j == back else 4):
                    ring_copy(a, back, t, j).wait_send()
        return 0

    lax.fori_loop(0, 4, drain, 0)


COPIES = 56
VMEM_BYTES = 62 * 1024 * 1024


def emit(a, b, c, d, a_out, b_out, c_out, d_out, a_buf, b_buf, c_buf, d_buf, sem):
    steps = ((a, a_buf, a_out), (b, b_buf, b_out), (c, c_buf, c_out), (d, d_buf, d_out))
    loads = [pltpu.make_async_copy(t[0], t[1], sem.at[0, n]) for n, t in enumerate(steps)]
    stores = [pltpu.make_async_copy(t[1], t[2], sem.at[1, n]) for n, t in enumerate(steps)]
    for copy in loads:
        copy.start()
    for load, store in zip(loads, stores):
        load.wait()
        store.start()
    for copy in stores:
        copy.wait()


def per_device(queries, key_vectors, value_vectors, group_order, doc_lengths, out_grad, out_weight):
    hbm = pl.BlockSpec(memory_space=pl.ANY)
    local = pltpu.VMEM((HALF, 2 * HD), BF16)
    pair_f32 = pltpu.VMEM((PAIR, HD), F32)
    pair_int = pltpu.VMEM((PAIR, HD), jnp.int32)
    results = pl.pallas_call(
        kernel,
        out_shape=(
            jax.ShapeDtypeStruct((HALF, 512), BF16),
            jax.ShapeDtypeStruct((HALF, 2 * HD), BF16),
            jax.ShapeDtypeStruct((HALF, 2 * HD), BF16),
            jax.ShapeDtypeStruct((HALF, 2 * HD), BF16),
        ),
        in_specs=[hbm] * 7,
        out_specs=(hbm, hbm, hbm, hbm),
        scratch_shapes=[
            pltpu.SMEM((64,), jnp.int32),
            pltpu.SMEM((DOCS,), jnp.int32),
            local, local, local,
            pltpu.VMEM((HALF, 512), BF16),
            pltpu.VMEM((3, HALF, 2 * HD), BF16),
            pltpu.VMEM((4, 9 * BLK, HD), BF16),
            pltpu.VMEM((HALF, 4096), BF16),
            pltpu.VMEM((HALF, 4096), BF16),
            pltpu.VMEM((NK, HALF, 512), BF16),
            pltpu.VMEM((HALF, HALF), BF16),
            pltpu.VMEM((HALF, HALF), F32),
            pltpu.VMEM((BLK, HD), BF16),
            pltpu.VMEM((NK, HALF, HALF), BF16),
            pair_int, pair_int, pair_int,
            pair_f32, pair_f32, pair_f32, pair_f32, pair_f32, pair_f32, pair_f32, pair_f32,
            pltpu.VMEM((BLK, HD), BF16),
            pltpu.VMEM((BLK, HD), BF16),
            pltpu.VMEM((1, 8, BLK), F32),
            pltpu.VMEM((8, BLK), F32),
            pltpu.VMEM((NZ, 8, BLK), F32),
            pltpu.VMEM((8, BLK), F32),
            pltpu.VMEM((3, 3, HALF, HD), BF16),
            pltpu.VMEM((3, 3, HALF, HD), BF16),
            pltpu.SemaphoreType.DMA((COPIES,)),
            pltpu.SemaphoreType.DMA((COPIES,)),
            pltpu.SemaphoreType.DMA((4, 2, 4, 2)),
            pltpu.SemaphoreType.DMA((4, 2, 4, 2)),
            pltpu.SemaphoreType.DMA((2, 4)),
            pltpu.SemaphoreType.DMA((2, 4)),
            pltpu.SemaphoreType.DMA((11,)),
        ],
        compiler_params=pltpu.CompilerParams(
            collective_id=0, has_side_effects=True, vmem_limit_bytes=VMEM_BYTES
        ),
        name="attention_grads",
    )(group_order, doc_lengths, queries, key_vectors, value_vectors, out_grad, out_weight)
    return pl.pallas_call(
        emit,
        out_shape=tuple(jax.ShapeDtypeStruct(r.shape, r.dtype) for r in results),
        in_specs=[pl.BlockSpec(memory_space=pl.ANY)] * 4,
        out_specs=(pl.BlockSpec(memory_space=pl.ANY),) * 4,
        scratch_shapes=[pltpu.VMEM(r.shape, r.dtype) for r in results]
        + [pltpu.SemaphoreType.DMA((2, 4))],
        compiler_params=pltpu.CompilerParams(vmem_limit_bytes=VMEM_BYTES),
        name="emit",
    )(*results)


def solution(mesh):
    return jax.shard_map(
        per_device,
        mesh=mesh,
        in_specs=(
            P("seq", "head"),
            P("seq", "head"),
            P("seq", "head"),
            P(),
            P(),
            P("seq", None),
            P("head", None),
        ),
        out_specs=(P("seq", "head"), P("seq", "head"), P("seq", "head"), P("seq", "head")),
        check_vma=False,
    )
```
